32 devices in a mesh: groups: 2 (over y), gx: 4 (over z), gy: 2 (over x), gz: 2 (over core).
Axes of the slice: x: 2, y: 2, z: 4, core: 2. Of those that a mesh axis runs over, the one named last changes fastest.
Arguments:
- parent: bfloat16 [160, 32, 1024], P('groups', 'gx', ('gy', 'gz')), parts along dimension 0, may hold values from -6 to 6
- nest: bfloat16 [160, 24, 1536], P('groups', 'gx', ('gy', 'gz')), parts along dimension 0, may hold values from -6 to 6
- nu_parent: float32 [80], replicated, may hold values from 0.03 to 0.24
- nu_nest: float32 [80], replicated, may hold values from 0.03 to 0.24
- relax: float32 [80], replicated, may hold values from 0.1 to 0.5
- feedback: float32 [80], replicated, may hold values from 0.3 to 1
- vert_mix: float32 [80, 80], replicated, may hold values from -1 to 1
- fp_owner: int32 [4, 4, 256, 1], P('gx', ('gy', 'gz')), may hold values from 0 to 3; in each aligned block of 256 rows (0 to 255, 256 to 511, ..., all dimensions but the last counted through in order) at most 256 rows name the same one
- fp_cell: int32 [4, 4, 256], P('gx', ('gy', 'gz')), may hold values from 0 to 2047
- nest_of: int32 [24], replicated, may hold values from 0 to 2, as said below
Outputs:
- parent_out: bfloat16 [160, 32, 1024], P('groups', 'gx', ('gy', 'gz')), parts along dimension 0
- nest_out: bfloat16 [160, 24, 1536], P('groups', 'gx', ('gy', 'gz')), parts along dimension 0
The draws below stay inside these ranges and needn't reach their ends.
There are 2 independent parts, one for each index of `groups`. The reference program is written for one: setup_inputs(seed, part) draws one part's arguments, and reference() takes and returns one part's arrays. A program takes and returns all parts, laid end to end along the dimension named above; an argument that names none is the same for every part. Nothing has to cross between parts.
Inputs may be any that keep to these rules, and one draw needn't show every extreme that they name: `fp_owner`: within the 256 blocks of one nest tile no parent tile is named more than 256 times; in some nest tiles one is named exactly 256 times. `nest_of`: never falls along the rows; every nest holds one or more rows; nest 1 holds rows 11 and 12.
All inputs are finite; a program needn't handle non-finite values.
Results may differ from the reference program's by a relative error of at most 0.0033.
Values may be sent and summed in bfloat16 or wider, within the bound.
A program may use at most 64 MiB of HBM per device.

```python
import math
import jax
import jax.numpy as jnp
import numpy as np
from jax import lax

LEV = 80
PCX = 8
PCY = 256
BCX = 2
BCY = 128
NYT = 4
REQ = 256
CAP = 256
PX = 32
PY = 1024
NX = 24
NY = 1536
N_GX = 4
N_GY = 2
N_GZ = 2


def draw_vert_mix(key, part):
    first_key, second_key = jax.random.split(jax.random.fold_in(key, 7))
    spread = jax.random.normal(first_key, (LEV, LEV), jnp.float32) * (0.25 / LEV ** 0.5)
    spread = jnp.clip(spread, -0.2, 0.2)
    diagonal = jax.random.uniform(second_key, (LEV,), jnp.float32, 0.5, 0.7)
    identity = jnp.eye(LEV, dtype=jnp.float32)
    return (spread * (1.0 - identity) + identity * diagonal[:, None]).astype(jnp.float32)


def draw_nest_of(key, part):
    first_key, second_key = jax.random.split(jax.random.fold_in(key, 11))
    start_one = jax.random.randint(first_key, (), 1, NX // 2, jnp.int32)
    start_two = jax.random.randint(second_key, (), NX // 2 + 1, NX, jnp.int32)
    rows_all = jnp.arange(NX, dtype=jnp.int32)
    return ((rows_all >= start_one).astype(jnp.int32) + (rows_all >= start_two).astype(jnp.int32)).astype(jnp.int32)


def place_ends(result, own_key, least, largest):
    index_at = [jax.random.randint(jax.random.fold_in(own_key, axis), (), 0, length) for axis, length in enumerate(result.shape)]
    longest = result.shape.index(max(result.shape))
    beside = index_at[:longest] + [(index_at[longest] + 1) % result.shape[longest]] + index_at[longest + 1:]
    return result.at[tuple(index_at)].set(least).at[tuple(beside)].set(largest)


def shard_levels(rng, dims, shards, smallest, top_value):
    level, own = 1.0, jax.random.fold_in(rng, 6)
    for position, shards_of in shards:
        draws = jnp.exp(jax.random.uniform(jax.random.fold_in(own, position), (shards_of,), jnp.float32, smallest / len(shards), top_value / len(shards)))
        level = level * jnp.repeat(draws, dims[position] // shards_of).reshape([-1 if axis == position else 1 for axis in range(len(dims))])
    return level


def shared_out(own_key, own, number, rows, number_of, top, reach, slope):
    ranking = jax.random.permutation(own_key, number_of)
    heavy_load, common = shares(number_of, rows * top, reach, slope, True), shares(number_of, rows * top, reach, slope, False)
    places = jnp.arange(number_of)

    def named(lengths, offset_by):
        used = int((lengths > 0).sum())
        fixed = max(1, used // 4)
        shifted = fixed + (places - fixed + offset_by * (used - fixed)) % max(1, number_of - fixed)
        return jnp.zeros((number_of,), jnp.int32).at[ranking[jnp.where(places < fixed, places, shifted)]].set(jnp.asarray(lengths, jnp.int32))

    lengths = jnp.where(number % 4 == 0, named(heavy_load, number // 4), named(common, number - number // 4 - 1))
    mixed = jax.random.permutation(jax.random.fold_in(own, 3), number_of)
    donor, receiver = mixed[0:number_of // 2 * 2:2], mixed[1:number_of // 2 * 2:2]
    slack = jnp.minimum(lengths[donor] - 1, reach - lengths[receiver]) // 2
    slack = jnp.where((donor == ranking[0]) | (receiver == ranking[0]) | (lengths[receiver] == 0), 0, jnp.maximum(slack, 0))
    shifted = jax.random.randint(jax.random.fold_in(own, 4), (number_of // 2,), 0, 1 << 20) % (slack + 1)
    lengths = lengths.at[donor].add(-shifted).at[receiver].add(shifted)
    items = jnp.searchsorted(jnp.cumsum(lengths), jnp.arange(rows * top), side="right").astype(jnp.int32)
    table = items.reshape(top, rows).T
    table = table[jax.random.permutation(jax.random.fold_in(own, 1), rows)]
    offset_by = jax.random.randint(jax.random.fold_in(own, 2), (rows, 1), 0, top)
    return jnp.take_along_axis(table, (jnp.arange(top)[None, :] + offset_by) % top, axis=1)


def shares(number_of, total, bound, skew, full):
    weights = [(1 << 20) // math.isqrt(rank ** skew) + 1 for rank in range(1, number_of + 1)]
    largest = bound if full else min(bound, max(-(-total // number_of), total * weights[0] // sum(weights)))
    least = 1 if total - largest >= number_of - 1 else 0
    counts, surplus = [largest] + [least] * (number_of - 1), total - largest - least * (number_of - 1)
    while surplus > 0:
        free = [i for i in range(1, number_of) if counts[i] < largest] or [i for i in range(1, number_of) if counts[i] < bound]
        mass, budget = sum([weights[i] for i in free]), surplus
        for i in free:
            extra = min(bound - counts[i], max(1, budget * weights[i] // mass), surplus)
            counts[i] = counts[i] + extra
            surplus = surplus - extra
    return np.array(counts)


def noise(key, dims, scale, reach, pieces=(), kind=jnp.bfloat16):
    drawn = jax.random.normal(key, dims, jnp.float32) * scale
    if len(pieces) > 0:
        drawn = shard_levels(key, dims, pieces, -0.22, 0.18) * drawn
    return jnp.clip(drawn, min=-reach, max=reach).astype(kind)


def setup_inputs(seed: int = 0, part: int = 0) -> dict:
    arg_keys = jax.random.split(jax.random.key(seed), 11)
    part_splits = jax.random.split(jax.random.fold_in(arg_keys[10], part), 11)
    parent = noise(part_splits[0], (LEV, PX, PY), 1.0, 6.0, ((1, 4), (2, 4)))
    nest = noise(part_splits[1], (LEV, NX, NY), 1.0, 6.0, ((1, 4), (2, 4)))
    nu_parent = jnp.clip(jnp.exp(jax.random.uniform(arg_keys[2], (LEV,), jnp.float32, math.log(0.03), math.log(0.24))), 0.03, 0.24)
    nu_nest = jnp.clip(jnp.exp(jax.random.uniform(arg_keys[3], (LEV,), jnp.float32, math.log(0.03), math.log(0.24))), 0.03, 0.24)
    relax = jnp.clip(jnp.exp(jax.random.uniform(arg_keys[4], (LEV,), jnp.float32, math.log(0.1), math.log(0.5))), 0.1, 0.5)
    feedback = jnp.clip(jnp.exp(jax.random.uniform(arg_keys[5], (LEV,), jnp.float32, math.log(0.3), math.log(1.0))), 0.3, 1.0)
    vert_mix = draw_vert_mix(jax.random.fold_in(arg_keys[10], 71), part)
    fp_owner_keys = jax.random.split(jax.random.fold_in(arg_keys[7], 1), N_GX * NYT * REQ // REQ)
    fp_owner_turns = jax.random.permutation(jax.random.fold_in(arg_keys[7], 3), N_GX * NYT * REQ // REQ)
    fp_owner = jax.vmap(lambda own, number: shared_out(jax.random.fold_in(arg_keys[7], 2), own, number, REQ, N_GX, 1, CAP, 2))(fp_owner_keys, fp_owner_turns).reshape((N_GX, NYT, REQ, 1))
    fp_cell = place_ends(jax.random.randint(arg_keys[8], (N_GX, NYT, REQ), 0, PCX * PCY), jax.random.fold_in(arg_keys[8], 1), 0, (PCX * PCY) - 1).astype(jnp.int32)
    nest_of = draw_nest_of(jax.random.fold_in(arg_keys[10], 71), part)
    return dict(parent=parent, nest=nest, nu_parent=nu_parent, nu_nest=nu_nest, relax=relax, feedback=feedback, vert_mix=vert_mix, fp_owner=fp_owner, fp_cell=fp_cell, nest_of=nest_of)


def mix_levels(matrix, values):
    flat_values = values.reshape(values.shape[0], -1)
    mixed = jnp.dot(matrix, flat_values, precision=lax.Precision.HIGHEST, preferred_element_type=jnp.float32)
    return mixed.reshape(values.shape)


def laplace(padded, centre):
    return ((padded[:, 2:, 1:-1] + padded[:, :-2, 1:-1]) + padded[:, 1:-1, 2:]) + padded[:, 1:-1, :-2] - 4.0 * centre


def to_grid(values, tiles_y):
    shaped = values.reshape(N_GX, tiles_y, BCX, BCY).transpose(0, 2, 1, 3)
    return shaped.reshape(N_GX * BCX, tiles_y * BCY)


def reference(parent, nest, nu_parent, nu_nest, relax, feedback, vert_mix, fp_owner, fp_cell, nest_of):
    coarse = parent.astype(jnp.float32)
    padded = jnp.pad(coarse, ((0, 0), (1, 1), (1, 1)))
    stepped = mix_levels(vert_mix, coarse + nu_parent[:, None, None] * laplace(padded, coarse))
    tiles_y = N_GY * N_GZ
    owners = fp_owner[..., 0].astype(jnp.int32)
    tile_index = jnp.arange(tiles_y, dtype=jnp.int32)[None, :, None]
    source_rows = to_grid(owners * PCX + fp_cell // PCY, tiles_y)
    source_cols = to_grid(tile_index * PCY + fp_cell % PCY, tiles_y)
    forcing_block = stepped[:, source_rows, source_cols]
    forcing_full = jnp.repeat(jnp.repeat(forcing_block, 3, axis=1), 3, axis=2)
    segment = nest_of.astype(jnp.int32)
    same_nest = (segment[1:] == segment[:-1]).astype(jnp.float32)
    zero_edge = jnp.zeros((1,), jnp.float32)
    left_ok = jnp.concatenate([zero_edge, same_nest])
    right_ok = jnp.concatenate([same_nest, zero_edge])
    nest_state = nest.astype(jnp.float32)
    for turn_no in range(3):
        padded = jnp.pad(nest_state, ((0, 0), (1, 1), (1, 1)))
        stencil_sum = ((padded[:, 2:, 1:-1] * right_ok[None, :, None] + padded[:, :-2, 1:-1] * left_ok[None, :, None]) + padded[:, 1:-1, 2:]) + padded[:, 1:-1, :-2] - 4.0 * nest_state
        moved = nest_state + nu_nest[:, None, None] * stencil_sum
        moved = moved + relax[:, None, None] * (forcing_full - moved)
        nest_state = mix_levels(vert_mix, moved)
    blocks = nest_state.reshape(LEV, N_GX * BCX, 3, tiles_y * BCY, 3).mean(axis=(2, 4))
    nudge_gap = blocks - forcing_block
    returned = jnp.zeros_like(stepped).at[:, source_rows, source_cols].add(nudge_gap)
    parent_out = (stepped + feedback[:, None, None] * returned).astype(jnp.bfloat16)
    return parent_out, nest_state.astype(jnp.bfloat16)
```

```python
import functools

import jax
import jax.numpy as jnp
from jax import lax
from jax.experimental import pallas as pl
from jax.experimental.pallas import tpu as pltpu
from jax.sharding import PartitionSpec as P

MESH = pl.DeviceIdType.MESH
F32 = jnp.float32
BF16 = jnp.bfloat16
LOW, HIGH = 0, 1
TURNS = 3


def dot(a, b):
    return jnp.dot(a, b, preferred_element_type=F32)


def one_hot(mask):
    return jnp.where(mask, 1.0, 0.0).astype(BF16)


def split(x):
    high = x.astype(BF16)
    return high, (x - high.astype(F32)).astype(BF16)


def over(first, count, step):
    if count <= 8:
        for k in range(first, count):
            step(k)
    else:
        lax.fori_loop(first, count, lambda k, _: (step(k), 0)[1], 0)


def kernel(
    n_x, n_gy, n_gz,
    parent, nest, nu_p, nu_n, relax, feedback, vert_mix, owner, cell, nest_of,
    parent_out, nest_out,
    keys, prow, pcol, pcol_send, nrow, nrow_send, ncol, ncol_send,
    state, stepped, stepped_bf, answers, answers_send, means, lhs, pulled,
    row_s, row_r, col_s, col_r, key_s, key_r, ans_s, ans_r, mean_s, mean_r,
):
    prows, levels, pcols = parent.shape
    nrows, _, ncols = nest.shape
    brows, bcols = nrows // 3, ncols // 3
    blocks = brows * bcols
    total_rows = nest_of.shape[0]
    me = lax.axis_index("gx")
    tile = lax.axis_index("gy") * n_gz + lax.axis_index("gz")
    n_y = n_gy * n_gz

    def y_device(t):
        return {"gy": t // n_gz, "gz": t % n_gz}

    x_side = ((me > 0, {"gx": me - 1}), (me < n_x - 1, {"gx": me + 1}))
    y_side = ((tile > 0, y_device(tile - 1)), (tile < n_y - 1, y_device(tile + 1)))

    barrier = pltpu.get_barrier_semaphore()

    def greet(k):
        pl.semaphore_signal(
            barrier, inc=1, device_id={"gx": lax.rem(me + k, n_x)}, device_id_type=MESH
        )

    over(1, n_x, greet)
    for present, device in y_side:
        @pl.when(present)
        def _():
            pl.semaphore_signal(barrier, inc=1, device_id=device, device_id_type=MESH)

    lane128 = lax.broadcasted_iota(jnp.int32, (levels, 128), 1)

    def pack(columns):
        packed = jnp.zeros((levels, 128), F32)
        for r, column in enumerate(columns):
            packed = jnp.where(lane128 == r, column, packed)
        return packed.astype(BF16)

    def edges(rows, width):
        low = pack([rows[r][:, 0:1] for r in range(len(rows))])
        high = pack([rows[r][:, width - 1:width] for r in range(len(rows))])
        return low, high

    p = [parent[r].astype(F32) for r in range(prows)]
    for side, packed in enumerate(edges(p, pcols)):
        pcol_send[side] = packed
    s = [nest[r].astype(F32) for r in range(nrows)]
    for side, packed in enumerate(edges(s, ncols)):
        ncol_send[0, side] = packed
    key = owner[...] * (prows * pcols) + cell[...]
    keys[0] = jnp.broadcast_to(key, keys.shape[1:])

    for side in (LOW, HIGH):
        @pl.when(jnp.logical_not(x_side[side][0]))
        def _():
            prow[side] = jnp.zeros(prow.shape[1:], BF16)
            for turn in range(TURNS):
                nrow[turn, side] = jnp.zeros(nrow.shape[2:], BF16)

        @pl.when(jnp.logical_not(y_side[side][0]))
        def _():
            pcol[side] = jnp.zeros(pcol.shape[1:], BF16)
            for turn in range(TURNS):
                ncol[turn, side] = jnp.zeros(ncol.shape[2:], BF16)

    callers = n_x - 1 + sum(present.astype(jnp.int32) for present, _ in y_side)
    pl.semaphore_wait(barrier, callers)

    def copy(src, dst, send_sem, recv_sem, device):
        return pltpu.make_async_remote_copy(
            src_ref=src, dst_ref=dst, send_sem=send_sem, recv_sem=recv_sem,
            device_id=device, device_id_type=MESH,
        )

    def halo(sides, side, src, dst, send_sems, recv_sems, which, do):
        present, device = sides[side]

        @pl.when(present)
        def _():
            if do == "start":
                copy(src, dst(1 - side), send_sems.at[which, side],
                     recv_sems.at[which, 1 - side], device).start()
            elif do == "recv":
                copy(src, dst(side), send_sems.at[which, side],
                     recv_sems.at[which, side], device).wait_recv()
            else:
                copy(src, dst(1 - side), send_sems.at[which, side],
                     recv_sems.at[which, 1 - side], device).wait_send()

    def parent_halo(side, do):
        halo(x_side, side, parent.at[0 if side == LOW else prows - 1],
             lambda where: prow.at[where], row_s, row_r, 0, do)
        halo(y_side, side, pcol_send.at[side], lambda where: pcol.at[where], col_s, col_r, 0, do)

    def nest_halo(turn, side, do, kinds=("x", "y")):
        if "x" in kinds:
            if turn == 0:
                src = nest.at[0 if side == LOW else nrows - 1]
            else:
                src = nrow_send.at[turn - 1, side]
            halo(x_side, side, src, lambda where: nrow.at[turn, where], row_s, row_r, 1 + turn, do)
        if "y" in kinds:
            halo(y_side, side, ncol_send.at[turn, side], lambda where: ncol.at[turn, where],
                 col_s, col_r, 1 + turn, do)

    def peer(k):
        return {"gx": lax.rem(me + k, n_x)}

    def key_copy(k):
        return copy(keys.at[0], keys.at[k], key_s.at[k], key_r.at[k], peer(k))

    def answer_copy(k):
        return copy(answers_send.at[k], answers.at[k], ans_s.at[k], ans_r.at[k],
                    {"gx": lax.rem(me + (n_x - k), n_x)})

    def mean_copy(k):
        return copy(means.at[0], means.at[k], mean_s.at[k], mean_r.at[k], peer(k))

    for side in (LOW, HIGH):
        parent_halo(side, "start")
    over(1, n_x, lambda k: key_copy(k).start())
    for side in (LOW, HIGH):
        nest_halo(0, side, "start")

    def level_column(ref):
        at = lax.broadcasted_iota(jnp.int32, (levels, levels), 0)
        across = lax.broadcasted_iota(jnp.int32, (levels, levels), 1)
        return jnp.sum(jnp.where(at == across, ref[...], 0.0), axis=1, keepdims=True)

    nu_parent_c, nu_nest_c = level_column(nu_p), level_column(nu_n)
    relax_c, feedback_c = level_column(relax), level_column(feedback)
    keep_c = 1.0 - relax_c

    m_high, m_low = split(vert_mix[...])
    wide_at = lax.broadcasted_iota(jnp.int32, (levels, 3 * levels), 0)
    wide_across = lax.broadcasted_iota(jnp.int32, (levels, 3 * levels), 1)
    place_high = one_hot((wide_across == wide_at) | (wide_across == wide_at + levels))
    place_low = one_hot(wide_across == wide_at + 2 * levels)
    lhs[...] = (dot(m_high, place_high) + dot(m_low, place_low)).astype(BF16)

    def mix(x):
        high, low = split(x)
        return dot(lhs[...], jnp.concatenate([high, low, high], axis=0))

    def beside(x, low, high, width):
        lane = lax.broadcasted_iota(jnp.int32, (levels, width), 1)
        before = jnp.where(lane == 0, low, pltpu.roll(x, 1, axis=1))
        after = jnp.where(lane == width - 1, high, pltpu.roll(x, width - 1, axis=1))
        return before + after

    for side in (LOW, HIGH):
        parent_halo(side, "recv")
    p_low, p_high = pcol[LOW].astype(F32), pcol[HIGH].astype(F32)
    for r in range(prows):
        centre = parent[r].astype(F32)
        above = (parent[r - 1] if r > 0 else prow[LOW]).astype(F32)
        below = (parent[r + 1] if r < prows - 1 else prow[HIGH]).astype(F32)
        around = above + below + beside(centre, p_low[:, r:r + 1], p_high[:, r:r + 1], pcols)
        out = mix(centre + nu_parent_c * (around - 4.0 * centre))
        stepped[r] = out
        stepped_bf[r * levels:(r + 1) * levels, :] = out.astype(BF16)

    parent_col = lax.broadcasted_iota(jnp.int32, (pcols, blocks), 0)
    shift = pcols.bit_length() - 1

    def places(k):
        here = keys[k, 0:1, :] - me * (prows * pcols)
        return lax.shift_right_arithmetic(here, shift), one_hot(parent_col == (here & (pcols - 1)))

    def serve(k):
        if not (isinstance(k, int) and k == 0):
            key_copy(k).wait_recv()
        row, hot = places(k)
        found = dot(stepped_bf[...], hot)
        total = jnp.zeros((levels, blocks), F32)
        for r in range(prows):
            total = jnp.where(row == r, found[r * levels:(r + 1) * levels], total)
        if isinstance(k, int) and k == 0:
            answers[0] = total.astype(BF16)
        else:
            answers_send[k] = total.astype(BF16)
            answer_copy(k).start()

    over(1, n_x, serve)
    serve(0)

    def weight(low_row):
        first = nest_of[lax.rem(low_row + total_rows, total_rows)]
        second = nest_of[lax.rem(low_row + 1, total_rows)]
        return jnp.where(first == second, 1.0, 0.0).astype(F32)

    weights = [weight(me * nrows + r - 1) for r in range(nrows + 1)]

    def diffuse(turn, get, put):
        low, high = ncol[turn, LOW].astype(F32), ncol[turn, HIGH].astype(F32)
        for r in range(nrows):
            centre = get(r)
            above = get(r - 1) if r > 0 else nrow[turn, LOW].astype(F32)
            below = get(r + 1) if r < nrows - 1 else nrow[turn, HIGH].astype(F32)
            around = (
                above * weights[r] + below * weights[r + 1]
                + beside(centre, low[:, r:r + 1], high[:, r:r + 1], ncols)
            )
            put(r, mix(keep_c * (centre + nu_nest_c * (around - 4.0 * centre))))

    for side in (LOW, HIGH):
        nest_halo(0, side, "recv")

    def put_state(r, value):
        state[0, r] = value

    diffuse(0, lambda r: nest[r].astype(F32), put_state)

    parent_row = lax.broadcasted_iota(jnp.int32, (16, blocks), 0)

    def count_step(k):
        row, hot = places(k)
        return lax.dot_general(
            one_hot(parent_row == row), hot, (((1,), (1,)), ((), ())), preferred_element_type=F32
        )

    forced = answers[0].astype(F32)
    if n_x <= 8:
        counts = count_step(0)
        for k in range(1, n_x):
            counts = counts + count_step(k)
        for k in range(1, n_x):
            answer_copy(k).wait_recv()
            forced = forced + answers[k].astype(F32)
    else:
        counts = lax.fori_loop(
            0, n_x, lambda k, t: t + count_step(k), jnp.zeros((16, pcols), F32))

        def collect(k, t):
            answer_copy(k).wait_recv()
            return t + answers[k].astype(F32)

        forced = lax.fori_loop(1, n_x, collect, forced)

    block_at = lax.broadcasted_iota(jnp.int32, (bcols, ncols), 0)
    cell_at = lax.broadcasted_iota(jnp.int32, (bcols, ncols), 1)
    spread = one_hot((cell_at >= 3 * block_at) & (cell_at < 3 * block_at + 3))
    spread2 = jnp.concatenate([spread, spread], axis=0)
    drive = mix(relax_c * forced)
    for a in range(brows):
        high, low = split(drive[:, a * bcols:(a + 1) * bcols])
        pulled[a] = dot(jnp.concatenate([high, low], axis=1), spread2)

    def send_rows(turn, r, value):
        if r == 0:
            nrow_send[turn - 1, LOW] = value.astype(BF16)
            nest_halo(turn, LOW, "start", ("x",))
        if r == nrows - 1:
            nrow_send[turn - 1, HIGH] = value.astype(BF16)
            nest_halo(turn, HIGH, "start", ("x",))

    def send_cols(turn, slot):
        rows = [state[slot, r] for r in range(nrows)]
        for side, packed in enumerate(edges(rows, ncols)):
            ncol_send[turn, side] = packed
            nest_halo(turn, side, "start", ("y",))

    for r in (0, nrows - 1, *range(1, nrows - 1)):
        value = state[0, r] + pulled[r // 3]
        state[0, r] = value
        send_rows(1, r, value)
    send_cols(1, 0)

    for turn in range(1, TURNS):
        for side in (LOW, HIGH):
            nest_halo(turn, side, "recv")
        now, later = (turn - 1) % 2, turn % 2

        def put_next(r, value):
            value = value + pulled[r // 3]
            state[later, r] = value
            if turn < TURNS - 1:
                send_rows(turn + 1, r, value)
            else:
                nest_out[r] = value.astype(BF16)

        diffuse(turn, lambda r: state[now, r], put_next)
        if turn < TURNS - 1:
            send_cols(turn + 1, later)

    last = (TURNS - 1) % 2
    for a in range(brows):
        summed = state[last, 3 * a] + state[last, 3 * a + 1] + state[last, 3 * a + 2]
        high, low = split(summed)
        both = lax.dot_general(
            jnp.concatenate([high, low], axis=0), spread,
            (((1,), (1,)), ((), ())), preferred_element_type=F32,
        )
        mean = (both[:levels] + both[levels:]) * (1.0 / 9.0)
        means[0, :, a * bcols:(a + 1) * bcols] = mean.astype(BF16)
    over(1, n_x, lambda k: mean_copy(k).start())

    def give(k, total):
        row, hot = places(k)
        mean = means[k].astype(F32)
        shared = jnp.concatenate(
            [jnp.where(row == r, mean, 0.0).astype(BF16) for r in range(prows)], axis=0
        )
        return total + lax.dot_general(
            shared, hot, (((1,), (1,)), ((), ())), preferred_element_type=F32)

    returned = give(0, jnp.zeros((prows * levels, pcols), F32))
    if n_x <= 8:
        for k in range(1, n_x):
            mean_copy(k).wait_recv()
            returned = give(k, returned)
    else:
        def give_next(k, total):
            mean_copy(k).wait_recv()
            return give(k, total)

        returned = lax.fori_loop(1, n_x, give_next, returned)
    for r in range(prows):
        own = stepped[r]
        back = returned[r * levels:(r + 1) * levels] - counts[r:r + 1, :] * own
        parent_out[r] = (own + feedback_c * back).astype(BF16)

    for side in (LOW, HIGH):
        parent_halo(side, "send")
        for turn in range(TURNS):
            nest_halo(turn, side, "send")

    def sent(k):
        key_copy(k).wait_send()
        answer_copy(k).wait_send()
        mean_copy(k).wait_send()

    over(1, n_x, sent)


def body(n_x, n_gy, n_gz, parent, nest, nu_p, nu_n, relax, feedback, vert_mix, owner, cell, nest_of):
    levels, prows, pcols = parent.shape
    _, nrows, ncols = nest.shape
    blocks = cell.size
    vmem = pl.BlockSpec(memory_space=pltpu.VMEM)
    smem = pl.BlockSpec(memory_space=pltpu.SMEM)
    dma = pltpu.SemaphoreType.DMA
    parent_out, nest_out = pl.pallas_call(
        functools.partial(kernel, n_x, n_gy, n_gz),
        out_shape=(
            jax.ShapeDtypeStruct((prows, levels, pcols), BF16),
            jax.ShapeDtypeStruct((nrows, levels, ncols), BF16),
        ),
        in_specs=[vmem] * 9 + [smem],
        out_specs=(vmem, vmem),
        scratch_shapes=[
            pltpu.VMEM((n_x, 8, blocks), jnp.int32),
            pltpu.VMEM((2, levels, pcols), BF16),
            pltpu.VMEM((2, levels, 128), BF16),
            pltpu.VMEM((2, levels, 128), BF16),
            pltpu.VMEM((TURNS, 2, levels, ncols), BF16),
            pltpu.VMEM((TURNS - 1, 2, levels, ncols), BF16),
            pltpu.VMEM((TURNS, 2, levels, 128), BF16),
            pltpu.VMEM((TURNS, 2, levels, 128), BF16),
            pltpu.VMEM((2, nrows, levels, ncols), F32),
            pltpu.VMEM((prows, levels, pcols), F32),
            pltpu.VMEM((prows * levels, pcols), BF16),
            pltpu.VMEM((n_x, levels, blocks), BF16),
            pltpu.VMEM((n_x, levels, blocks), BF16),
            pltpu.VMEM((n_x, levels, blocks), BF16),
            pltpu.VMEM((levels, 3 * levels), BF16),
            pltpu.VMEM((nrows // 3, levels, ncols), F32),
            dma((1 + TURNS, 2)), dma((1 + TURNS, 2)), dma((1 + TURNS, 2)), dma((1 + TURNS, 2)),
            dma((n_x,)), dma((n_x,)), dma((n_x,)), dma((n_x,)), dma((n_x,)), dma((n_x,)),
        ],
        compiler_params=pltpu.CompilerParams(
            collective_id=0, has_side_effects=True, vmem_limit_bytes=40 * 1024 * 1024
        ),
    )(
        parent.transpose(1, 0, 2), nest.transpose(1, 0, 2),
        nu_p.reshape(1, -1), nu_n.reshape(1, -1), relax.reshape(1, -1), feedback.reshape(1, -1),
        vert_mix, owner.reshape(1, -1), cell.reshape(1, -1), nest_of,
    )
    return parent_out.transpose(1, 0, 2), nest_out.transpose(1, 0, 2)


def solution(mesh):
    sizes = mesh.shape
    grid = P("groups", "gx", ("gy", "gz"))
    placed = (
        grid, grid, P(), P(), P(), P(), P(),
        P("gx", ("gy", "gz"), None, None), P("gx", ("gy", "gz"), None), P(),
    )
    return jax.shard_map(
        functools.partial(body, sizes["gx"], sizes["gy"], sizes["gz"]),
        mesh=mesh,
        in_specs=placed,
        out_specs=(grid, grid),
        check_vma=False,
    )
```

```python
import functools

import jax
import jax.numpy as jnp
from jax import lax
from jax.experimental import pallas as pl
from jax.experimental.pallas import tpu as pltpu
from jax.sharding import PartitionSpec as P

MESH = pl.DeviceIdType.MESH
F32 = jnp.float32
BF16 = jnp.bfloat16
LOW, HIGH = 0, 1
TURNS = 3


def dot(a, b):
    return jnp.dot(a, b, preferred_element_type=F32)


def one_hot(mask):
    return jnp.where(mask, 1.0, 0.0).astype(BF16)


def split(x):
    high = x.astype(BF16)
    return high, (x - high.astype(F32)).astype(BF16)


def over(first, count, step):
    if count <= 8:
        for k in range(first, count):
            step(k)
    else:
        lax.fori_loop(first, count, lambda k, _: (step(k), 0)[1], 0)


def kernel(
    n_x, n_gy, n_gz,
    parent, nest, nu_p, nu_n, relax, feedback, vert_mix, owner, cell, nest_of,
    parent_out, nest_out,
    keys, prow, pcol, pcol_send, nrow, nrow_send, ncol, ncol_send,
    state, stepped, stepped_bf, answers, answers_send, means, lhs, pulled, back,
    row_s, row_r, col_s, col_r, key_s, key_r, ans_s, ans_r, mean_s, mean_r,
):
    prows, levels, pcols = parent.shape
    nrows, _, ncols = nest.shape
    brows, bcols = nrows // 3, ncols // 3
    blocks = brows * bcols
    total_rows = nest_of.shape[0]
    me = lax.axis_index("gx")
    tile = lax.axis_index("gy") * n_gz + lax.axis_index("gz")
    n_y = n_gy * n_gz

    def y_device(t):
        return {"gy": t // n_gz, "gz": t % n_gz}

    x_side = ((me > 0, {"gx": me - 1}), (me < n_x - 1, {"gx": me + 1}))
    y_side = ((tile > 0, y_device(tile - 1)), (tile < n_y - 1, y_device(tile + 1)))

    barrier = pltpu.get_barrier_semaphore()

    def greet(k):
        pl.semaphore_signal(
            barrier, inc=1, device_id={"gx": lax.rem(me + k, n_x)}, device_id_type=MESH
        )

    over(1, n_x, greet)
    for present, device in y_side:
        @pl.when(present)
        def _():
            pl.semaphore_signal(barrier, inc=1, device_id=device, device_id_type=MESH)

    lane128 = lax.broadcasted_iota(jnp.int32, (levels, 128), 1)

    def pack(columns):
        packed = jnp.zeros((levels, 128), F32)
        for r, column in enumerate(columns):
            packed = jnp.where(lane128 == r, column, packed)
        return packed

    def edges(rows, width):
        low = pack([rows[r][:, 0:1] for r in range(len(rows))])
        high = pack([rows[r][:, width - 1:width] for r in range(len(rows))])
        return low, high

    p = [parent[r].astype(F32) for r in range(prows)]
    for side, packed in enumerate(edges(p, pcols)):
        pcol_send[side] = packed.astype(BF16)
    s = [nest[r].astype(F32) for r in range(nrows)]
    for side, packed in enumerate(edges(s, ncols)):
        ncol_send[0, side] = packed.astype(BF16)
    key = owner[...] * (prows * pcols) + cell[...]
    keys[0] = jnp.broadcast_to(key, keys.shape[1:])

    for side in (LOW, HIGH):
        @pl.when(jnp.logical_not(x_side[side][0]))
        def _():
            prow[side] = jnp.zeros(prow.shape[1:], BF16)
            for turn in range(TURNS):
                nrow[turn, side] = jnp.zeros(nrow.shape[2:], BF16)

        @pl.when(jnp.logical_not(y_side[side][0]))
        def _():
            pcol[side] = jnp.zeros(pcol.shape[1:], BF16)
            for turn in range(TURNS):
                ncol[turn, side] = jnp.zeros(ncol.shape[2:], BF16)

    callers = n_x - 1 + sum(present.astype(jnp.int32) for present, _ in y_side)
    pl.semaphore_wait(barrier, callers)

    def copy(src, dst, send_sem, recv_sem, device):
        return pltpu.make_async_remote_copy(
            src_ref=src, dst_ref=dst, send_sem=send_sem, recv_sem=recv_sem,
            device_id=device, device_id_type=MESH,
        )

    def halo(sides, side, src, dst, send_sems, recv_sems, which, do):
        present, device = sides[side]

        @pl.when(present)
        def _():
            if do == "start":
                copy(src, dst(1 - side), send_sems.at[which, side],
                     recv_sems.at[which, 1 - side], device).start()
            elif do == "recv":
                copy(src, dst(side), send_sems.at[which, side],
                     recv_sems.at[which, side], device).wait_recv()
            else:
                copy(src, dst(1 - side), send_sems.at[which, side],
                     recv_sems.at[which, 1 - side], device).wait_send()

    def parent_halo(side, do):
        halo(x_side, side, parent.at[0 if side == LOW else prows - 1],
             lambda where: prow.at[where], row_s, row_r, 0, do)
        halo(y_side, side, pcol_send.at[side], lambda where: pcol.at[where], col_s, col_r, 0, do)

    def nest_halo(turn, side, do, kinds=("x", "y")):
        if "x" in kinds:
            if turn == 0:
                src = nest.at[0 if side == LOW else nrows - 1]
            else:
                src = nrow_send.at[turn - 1, side]
            halo(x_side, side, src, lambda where: nrow.at[turn, where], row_s, row_r, 1 + turn, do)
        if "y" in kinds:
            halo(y_side, side, ncol_send.at[turn, side], lambda where: ncol.at[turn, where],
                 col_s, col_r, 1 + turn, do)

    def peer(k):
        return {"gx": lax.rem(me + k, n_x)}

    def key_copy(k):
        return copy(keys.at[0], keys.at[k], key_s.at[k], key_r.at[k], peer(k))

    def answer_copy(k):
        return copy(answers_send.at[k], answers.at[k], ans_s.at[k], ans_r.at[k],
                    {"gx": lax.rem(me + (n_x - k), n_x)})

    def mean_copy(k):
        return copy(means.at[0], means.at[k], mean_s.at[k], mean_r.at[k], peer(k))

    for side in (LOW, HIGH):
        parent_halo(side, "start")
    over(1, n_x, lambda k: key_copy(k).start())
    for side in (LOW, HIGH):
        nest_halo(0, side, "start")

    def level_column(ref):
        at = lax.broadcasted_iota(jnp.int32, (levels, levels), 0)
        across = lax.broadcasted_iota(jnp.int32, (levels, levels), 1)
        return jnp.sum(jnp.where(at == across, ref[...], 0.0), axis=1, keepdims=True)

    nu_parent_c, nu_nest_c = level_column(nu_p), level_column(nu_n)
    relax_c, feedback_c = level_column(relax), level_column(feedback)
    keep_c = 1.0 - relax_c

    m_high, m_low = split(vert_mix[...])
    wide_at = lax.broadcasted_iota(jnp.int32, (levels, 3 * levels), 0)
    wide_across = lax.broadcasted_iota(jnp.int32, (levels, 3 * levels), 1)
    place_high = one_hot((wide_across == wide_at) | (wide_across == wide_at + levels))
    place_low = one_hot(wide_across == wide_at + 2 * levels)
    lhs[...] = (dot(m_high, place_high) + dot(m_low, place_low)).astype(BF16)

    def mix(x):
        high, low = split(x)
        return dot(lhs[...], jnp.concatenate([high, low, high], axis=0))

    def inside(x, width):
        lane = lax.broadcasted_iota(jnp.int32, (levels, width), 1)
        before = jnp.where(lane == 0, 0.0, pltpu.roll(x, 1, axis=1))
        after = jnp.where(lane == width - 1, 0.0, pltpu.roll(x, width - 1, axis=1))
        return before + after

    def halo_matrix(scale):
        high, low = split(vert_mix[...] * scale)
        at = lax.broadcasted_iota(jnp.int32, (levels, 2 * levels), 0)
        across = lax.broadcasted_iota(jnp.int32, (levels, 2 * levels), 1)
        return (
            dot(high, one_hot(across == at)) + dot(low, one_hot(across == at + levels))
        ).astype(BF16)

    parent_lhs = halo_matrix(nu_p[...])
    nest_lhs = halo_matrix(nu_n[...] * (1.0 - relax[...]))

    def from_halos(matrix, rows, cols):
        halos = jnp.concatenate([rows[LOW], rows[HIGH], cols[LOW], cols[HIGH]], axis=1)
        added = dot(matrix, jnp.concatenate([halos, halos], axis=0))
        width = rows.shape[-1]
        return (
            added[:, :width], added[:, width:2 * width],
            added[:, 2 * width:2 * width + 128], added[:, 2 * width + 128:],
        )

    def add_cols(target, r, width, low, high):
        target[:, :128] = target[:, :128] + jnp.where(lane128 == 0, low[:, r:r + 1], 0.0)
        target[:, width - 128:] = target[:, width - 128:] + jnp.where(
            lane128 == 127, high[:, r:r + 1], 0.0)

    for r in range(prows):
        centre = parent[r].astype(F32)
        around = inside(centre, pcols)
        if r > 0:
            around = around + parent[r - 1].astype(F32)
        if r < prows - 1:
            around = around + parent[r + 1].astype(F32)
        stepped[r] = mix(centre + nu_parent_c * (around - 4.0 * centre))
    for side in (LOW, HIGH):
        parent_halo(side, "recv")
    row_low, row_high, col_low, col_high = from_halos(parent_lhs, prow, pcol)
    stepped[0] = stepped[0] + row_low
    stepped[prows - 1] = stepped[prows - 1] + row_high
    for r in range(prows):
        add_cols(stepped.at[r], r, pcols, col_low, col_high)
        stepped_bf[r * levels:(r + 1) * levels, :] = stepped[r].astype(BF16)

    parent_col = lax.broadcasted_iota(jnp.int32, (pcols, blocks), 0)
    shift = pcols.bit_length() - 1

    def row_of(k):
        return lax.shift_right_arithmetic(keys[k, 0:1, :] - me * (prows * pcols), shift)

    def places(k):
        return row_of(k), one_hot(parent_col == (keys[k, 0:1, :] & (pcols - 1)))

    parent_across = lax.broadcasted_iota(jnp.int32, (blocks, pcols), 1)

    def place_back(k):
        down = jnp.transpose(keys[k])[:, 0:1]
        back[k] = one_hot(parent_across == (down & (pcols - 1)))

    def serve(k):
        if not (isinstance(k, int) and k == 0):
            key_copy(k).wait_recv()
        row, hot = places(k)
        found = dot(stepped_bf[...], hot)
        total = jnp.zeros((levels, blocks), F32)
        for r in range(prows):
            total = jnp.where(row == r, found[r * levels:(r + 1) * levels], total)
        if isinstance(k, int) and k == 0:
            answers[0] = total.astype(BF16)
        else:
            answers_send[k] = total.astype(BF16)
            answer_copy(k).start()

    over(1, n_x, serve)
    serve(0)

    def weight(low_row):
        first = nest_of[lax.rem(low_row + total_rows, total_rows)]
        second = nest_of[lax.rem(low_row + 1, total_rows)]
        return jnp.where(first == second, 1.0, 0.0).astype(F32)

    weights = [weight(me * nrows + r - 1) for r in range(nrows + 1)]

    def diffuse(get, put):
        for r in range(nrows):
            centre = get(r)
            around = inside(centre, ncols)
            if r > 0:
                around = around + get(r - 1) * weights[r]
            if r < nrows - 1:
                around = around + get(r + 1) * weights[r + 1]
            put(r, mix(keep_c * (centre + nu_nest_c * (around - 4.0 * centre))))

    def nest_halos(turn):
        for side in (LOW, HIGH):
            nest_halo(turn, side, "recv")
        row_low, row_high, col_low, col_high = from_halos(nest_lhs, nrow.at[turn], ncol.at[turn])
        return row_low * weights[0], row_high * weights[nrows], col_low, col_high

    def put_state(r, value):
        state[0, r] = value

    diffuse(lambda r: nest[r].astype(F32), put_state)
    row_low, row_high, col_low, col_high = nest_halos(0)
    state[0, 0] = state[0, 0] + row_low
    state[0, nrows - 1] = state[0, nrows - 1] + row_high
    for r in range(nrows):
        add_cols(state.at[0, r], r, ncols, col_low, col_high)

    parent_row = lax.broadcasted_iota(jnp.int32, (16, blocks), 0)
    over(0, n_x, place_back)

    def count_step(k):
        return dot(one_hot(parent_row == row_of(k)), back[k])

    forced = answers[0].astype(F32)
    if n_x <= 8:
        counts = count_step(0)
        for k in range(1, n_x):
            counts = counts + count_step(k)
        for k in range(1, n_x):
            answer_copy(k).wait_recv()
            forced = forced + answers[k].astype(F32)
    else:
        counts = lax.fori_loop(
            0, n_x, lambda k, t: t + count_step(k), jnp.zeros((16, pcols), F32))

        def collect(k, t):
            answer_copy(k).wait_recv()
            return t + answers[k].astype(F32)

        forced = lax.fori_loop(1, n_x, collect, forced)

    block_at = lax.broadcasted_iota(jnp.int32, (bcols, ncols), 0)
    cell_at = lax.broadcasted_iota(jnp.int32, (bcols, ncols), 1)
    spread = one_hot((cell_at >= 3 * block_at) & (cell_at < 3 * block_at + 3))
    spread2 = jnp.concatenate([spread, spread], axis=0)
    drive = mix(relax_c * forced)
    for a in range(brows):
        high, low = split(drive[:, a * bcols:(a + 1) * bcols])
        pulled[a] = dot(jnp.concatenate([high, low], axis=1), spread2)

    def send_rows(turn, r, value):
        side = LOW if r == 0 else HIGH
        nrow_send[turn - 1, side] = value.astype(BF16)
        nest_halo(turn, side, "start", ("x",))

    for r in (0, nrows - 1, *range(1, nrows - 1)):
        value = state[0, r] + pulled[r // 3]
        state[0, r] = value
        if r in (0, nrows - 1):
            send_rows(1, r, value)
    for side, packed in enumerate(edges([state[0, r] for r in range(nrows)], ncols)):
        ncol_send[1, side] = packed.astype(BF16)
        nest_halo(1, side, "start", ("y",))

    for turn in range(1, TURNS):
        now, later = (turn - 1) % 2, turn % 2

        def put_next(r, value):
            state[later, r] = value + pulled[r // 3]

        diffuse(lambda r: state[now, r], put_next)
        ends = None
        if turn < TURNS - 1:
            ends = edges([state[later, r] for r in range(nrows)], ncols)
        row_low, row_high, col_low, col_high = nest_halos(turn)
        for r, added in ((0, row_low), (nrows - 1, row_high)):
            state[later, r] = state[later, r] + added
            add_cols(state.at[later, r], r, ncols, col_low, col_high)
            if turn < TURNS - 1:
                send_rows(turn + 1, r, state[later, r])
        if turn < TURNS - 1:
            for side, (end, at, own) in enumerate(
                zip(ends, (0, ncols - 1), (col_low, col_high))
            ):
                end = end + own
                end = end + jnp.where(lane128 == 0, row_low[:, at:at + 1], 0.0)
                end = end + jnp.where(lane128 == nrows - 1, row_high[:, at:at + 1], 0.0)
                ncol_send[turn + 1, side] = end.astype(BF16)
                nest_halo(turn + 1, side, "start", ("y",))
        for r in range(1, nrows - 1):
            add_cols(state.at[later, r], r, ncols, col_low, col_high)

    last = (TURNS - 1) % 2
    down_cell = lax.broadcasted_iota(jnp.int32, (ncols, bcols), 0)
    down_block = lax.broadcasted_iota(jnp.int32, (ncols, bcols), 1)
    gather_up = one_hot((down_cell >= 3 * down_block) & (down_cell < 3 * down_block + 3))
    for a in range(brows):
        summed = state[last, 3 * a] + state[last, 3 * a + 1] + state[last, 3 * a + 2]
        high, low = split(summed)
        both = dot(jnp.concatenate([high, low], axis=0), gather_up)
        mean = (both[:levels] + both[levels:]) * (1.0 / 9.0)
        means[0, :, a * bcols:(a + 1) * bcols] = mean.astype(BF16)
    over(1, n_x, lambda k: mean_copy(k).start())
    for r in range(nrows):
        nest_out[r] = state[last, r].astype(BF16)

    def give(k, total):
        row = row_of(k)
        mean = means[k].astype(F32)
        shared = jnp.concatenate(
            [jnp.where(row == r, mean, 0.0).astype(BF16) for r in range(prows)], axis=0
        )
        return total + dot(shared, back[k])

    for r in range(prows):
        stepped[r] = stepped[r] * (1.0 - feedback_c * counts[r:r + 1, :])
    returned = give(0, jnp.zeros((prows * levels, pcols), F32))
    if n_x <= 8:
        for k in range(1, n_x):
            mean_copy(k).wait_recv()
            returned = give(k, returned)
    else:
        def give_next(k, total):
            mean_copy(k).wait_recv()
            return give(k, total)

        returned = lax.fori_loop(1, n_x, give_next, returned)
    for r in range(prows):
        given = returned[r * levels:(r + 1) * levels]
        parent_out[r] = (stepped[r] + feedback_c * given).astype(BF16)

    for side in (LOW, HIGH):
        parent_halo(side, "send")
        for turn in range(TURNS):
            nest_halo(turn, side, "send")

    def sent(k):
        key_copy(k).wait_send()
        answer_copy(k).wait_send()
        mean_copy(k).wait_send()

    over(1, n_x, sent)


def body(n_x, n_gy, n_gz, parent, nest, nu_p, nu_n, relax, feedback, vert_mix, owner, cell, nest_of):
    levels, prows, pcols = parent.shape
    _, nrows, ncols = nest.shape
    blocks = cell.size
    vmem = pl.BlockSpec(memory_space=pltpu.VMEM)
    smem = pl.BlockSpec(memory_space=pltpu.SMEM)
    dma = pltpu.SemaphoreType.DMA
    parent_out, nest_out = pl.pallas_call(
        functools.partial(kernel, n_x, n_gy, n_gz),
        out_shape=(
            jax.ShapeDtypeStruct((prows, levels, pcols), BF16),
            jax.ShapeDtypeStruct((nrows, levels, ncols), BF16),
        ),
        in_specs=[vmem] * 9 + [smem],
        out_specs=(vmem, vmem),
        scratch_shapes=[
            pltpu.VMEM((n_x, 8, blocks), jnp.int32),
            pltpu.VMEM((2, levels, pcols), BF16),
            pltpu.VMEM((2, levels, 128), BF16),
            pltpu.VMEM((2, levels, 128), BF16),
            pltpu.VMEM((TURNS, 2, levels, ncols), BF16),
            pltpu.VMEM((TURNS - 1, 2, levels, ncols), BF16),
            pltpu.VMEM((TURNS, 2, levels, 128), BF16),
            pltpu.VMEM((TURNS, 2, levels, 128), BF16),
            pltpu.VMEM((2, nrows, levels, ncols), F32),
            pltpu.VMEM((prows, levels, pcols), F32),
            pltpu.VMEM((prows * levels, pcols), BF16),
            pltpu.VMEM((n_x, levels, blocks), BF16),
            pltpu.VMEM((n_x, levels, blocks), BF16),
            pltpu.VMEM((n_x, levels, blocks), BF16),
            pltpu.VMEM((levels, 3 * levels), BF16),
            pltpu.VMEM((nrows // 3, levels, ncols), F32),
            pltpu.VMEM((n_x, blocks, pcols), BF16),
            dma((1 + TURNS, 2)), dma((1 + TURNS, 2)), dma((1 + TURNS, 2)), dma((1 + TURNS, 2)),
            dma((n_x,)), dma((n_x,)), dma((n_x,)), dma((n_x,)), dma((n_x,)), dma((n_x,)),
        ],
        compiler_params=pltpu.CompilerParams(
            collective_id=0, has_side_effects=True, vmem_limit_bytes=40 * 1024 * 1024
        ),
    )(
        parent.transpose(1, 0, 2), nest.transpose(1, 0, 2),
        nu_p.reshape(1, -1), nu_n.reshape(1, -1), relax.reshape(1, -1), feedback.reshape(1, -1),
        vert_mix, owner.reshape(1, -1), cell.reshape(1, -1), nest_of,
    )
    return parent_out.transpose(1, 0, 2), nest_out.transpose(1, 0, 2)


def solution(mesh):
    sizes = mesh.shape
    grid = P("groups", "gx", ("gy", "gz"))
    placed = (
        grid, grid, P(), P(), P(), P(), P(),
        P("gx", ("gy", "gz"), None, None), P("gx", ("gy", "gz"), None), P(),
    )
    return jax.shard_map(
        functools.partial(body, sizes["gx"], sizes["gy"], sizes["gz"]),
        mesh=mesh,
        in_specs=placed,
        out_specs=(grid, grid),
        check_vma=False,
    )
```

```python
import functools

import jax
import jax.numpy as jnp
from jax import lax
from jax.experimental import pallas as pl
from jax.experimental.pallas import tpu as pltpu
from jax.sharding import PartitionSpec as P

MESH = pl.DeviceIdType.MESH
F32 = jnp.float32
BF16 = jnp.bfloat16
LOW, HIGH = 0, 1
TURNS = 3


def dot(a, b):
    return jnp.dot(a, b, preferred_element_type=F32)


def one_hot(mask):
    return jnp.where(mask, 1.0, 0.0).astype(BF16)


def split(x):
    high = x.astype(BF16)
    return high, (x - high.astype(F32)).astype(BF16)


def over(first, count, step):
    if count <= 8:
        for k in range(first, count):
            step(k)
    else:
        lax.fori_loop(first, count, lambda k, _: (step(k), 0)[1], 0)


def kernel(
    n_x, n_gy, n_gz,
    parent_h, nest_h, nu_p_h, nu_n_h, relax_h, feedback_h, vert_mix_h, owner_h, cell_h, nest_of_h,
    parent_out, nest_out_h,
    parent_n, nest, nu_p, nu_n, relax, feedback, vert_mix, owner, cell, nest_of, turned, parent,
    in_sem, nest_out, out_sem,
    keys, prow, pcol, pcol_send, nrow, nrow_send, ncol, ncol_send,
    state, stepped, stepped_bf, answers, answers_send, means, lhs, pulled, back,
    row_s, row_r, col_s, col_r, key_s, key_r, ans_s, ans_r, mean_s, mean_r,
):
    loads = [
        pltpu.make_async_copy(src, dst, in_sem.at[i])
        for i, (src, dst) in enumerate((
            (parent_h, parent_n), (nest_h, nest), (owner_h, owner), (cell_h, cell),
            (vert_mix_h, vert_mix), (nu_p_h, nu_p), (nu_n_h, nu_n), (relax_h, relax),
            (feedback_h, feedback), (nest_of_h, nest_of),
        ))
    ]
    for load in loads:
        load.start()
    prows, levels, pcols = parent.shape
    nrows, _, ncols = nest.shape
    brows, bcols = nrows // 3, ncols // 3
    blocks = brows * bcols
    total_rows = nest_of.shape[0]
    me = lax.axis_index("gx")
    tile = lax.axis_index("gy") * n_gz + lax.axis_index("gz")
    n_y = n_gy * n_gz

    def y_device(t):
        return {"gy": t // n_gz, "gz": t % n_gz}

    x_side = ((me > 0, {"gx": me - 1}), (me < n_x - 1, {"gx": me + 1}))
    y_side = ((tile > 0, y_device(tile - 1)), (tile < n_y - 1, y_device(tile + 1)))

    barrier = pltpu.get_barrier_semaphore()

    def greet(k):
        pl.semaphore_signal(
            barrier, inc=1, device_id={"gx": lax.rem(me + k, n_x)}, device_id_type=MESH
        )

    over(1, n_x, greet)
    for present, device in y_side:
        @pl.when(present)
        def _():
            pl.semaphore_signal(barrier, inc=1, device_id=device, device_id_type=MESH)

    lane128 = lax.broadcasted_iota(jnp.int32, (levels, 128), 1)

    def pack(columns):
        packed = jnp.zeros((levels, 128), F32)
        for r, column in enumerate(columns):
            packed = jnp.where(lane128 == r, column, packed)
        return packed

    def edges(rows, width):
        low = pack([rows[r][:, 0:1] for r in range(len(rows))])
        high = pack([rows[r][:, width - 1:width] for r in range(len(rows))])
        return low, high

    for load in loads:
        load.wait()
    whole = parent_n[...].astype(F32)
    p = []
    for h in range(pcols // 128):
        turned[h] = whole[:, :, h * 128:(h + 1) * 128].reshape(levels * prows, 128)
    for r in range(prows):
        row = jnp.concatenate(
            [turned[h, pl.ds(r, levels, stride=prows), :] for h in range(pcols // 128)], axis=1
        )
        parent[r] = row.astype(BF16)
        p.append(row)
    for side, packed in enumerate(edges(p, pcols)):
        pcol_send[side] = packed.astype(BF16)
    s = [nest[r].astype(F32) for r in range(nrows)]
    for side, packed in enumerate(edges(s, ncols)):
        ncol_send[0, side] = packed.astype(BF16)
    key = owner[...] * (prows * pcols) + cell[...]
    keys[0] = jnp.broadcast_to(key, keys.shape[1:])

    for side in (LOW, HIGH):
        @pl.when(jnp.logical_not(x_side[side][0]))
        def _():
            prow[side] = jnp.zeros(prow.shape[1:], BF16)
            for turn in range(TURNS):
                nrow[turn, side] = jnp.zeros(nrow.shape[2:], BF16)

        @pl.when(jnp.logical_not(y_side[side][0]))
        def _():
            pcol[side] = jnp.zeros(pcol.shape[1:], BF16)
            for turn in range(TURNS):
                ncol[turn, side] = jnp.zeros(ncol.shape[2:], BF16)

    def level_column(ref):
        at = lax.broadcasted_iota(jnp.int32, (levels, levels), 0)
        across = lax.broadcasted_iota(jnp.int32, (levels, levels), 1)
        return jnp.sum(jnp.where(at == across, ref[...], 0.0), axis=1, keepdims=True)

    nu_parent_c, nu_nest_c = level_column(nu_p), level_column(nu_n)
    relax_c, feedback_c = level_column(relax), level_column(feedback)
    keep_c = 1.0 - relax_c

    m_high, m_low = split(vert_mix[...])
    wide_at = lax.broadcasted_iota(jnp.int32, (levels, 3 * levels), 0)
    wide_across = lax.broadcasted_iota(jnp.int32, (levels, 3 * levels), 1)
    place_high = one_hot((wide_across == wide_at) | (wide_across == wide_at + levels))
    place_low = one_hot(wide_across == wide_at + 2 * levels)
    lhs[...] = (dot(m_high, place_high) + dot(m_low, place_low)).astype(BF16)

    def mix(x):
        high, low = split(x)
        return dot(lhs[...], jnp.concatenate([high, low, high], axis=0))

    def inside(x, width):
        lane = lax.broadcasted_iota(jnp.int32, (levels, width), 1)
        before = jnp.where(lane == 0, 0.0, pltpu.roll(x, 1, axis=1))
        after = jnp.where(lane == width - 1, 0.0, pltpu.roll(x, width - 1, axis=1))
        return before + after

    def halo_matrix(scale):
        high, low = split(vert_mix[...] * scale)
        at = lax.broadcasted_iota(jnp.int32, (levels, 2 * levels), 0)
        across = lax.broadcasted_iota(jnp.int32, (levels, 2 * levels), 1)
        return (
            dot(high, one_hot(across == at)) + dot(low, one_hot(across == at + levels))
        ).astype(BF16)

    parent_lhs = halo_matrix(nu_p[...])
    nest_lhs = halo_matrix(nu_n[...] * (1.0 - relax[...]))

    def from_halos(matrix, rows, cols):
        halos = jnp.concatenate([rows[LOW], rows[HIGH], cols[LOW], cols[HIGH]], axis=1)
        added = dot(matrix, jnp.concatenate([halos, halos], axis=0))
        width = rows.shape[-1]
        return (
            added[:, :width], added[:, width:2 * width],
            added[:, 2 * width:2 * width + 128], added[:, 2 * width + 128:],
        )

    def add_cols(target, r, width, low, high):
        target[:, :128] = target[:, :128] + jnp.where(lane128 == 0, low[:, r:r + 1], 0.0)
        target[:, width - 128:] = target[:, width - 128:] + jnp.where(
            lane128 == 127, high[:, r:r + 1], 0.0)

    callers = n_x - 1 + sum(present.astype(jnp.int32) for present, _ in y_side)
    pl.semaphore_wait(barrier, callers)

    def copy(src, dst, send_sem, recv_sem, device):
        return pltpu.make_async_remote_copy(
            src_ref=src, dst_ref=dst, send_sem=send_sem, recv_sem=recv_sem,
            device_id=device, device_id_type=MESH,
        )

    def halo(sides, side, src, dst, send_sems, recv_sems, which, do):
        present, device = sides[side]

        @pl.when(present)
        def _():
            if do == "start":
                copy(src, dst(1 - side), send_sems.at[which, side],
                     recv_sems.at[which, 1 - side], device).start()
            elif do == "recv":
                copy(src, dst(side), send_sems.at[which, side],
                     recv_sems.at[which, side], device).wait_recv()
            else:
                copy(src, dst(1 - side), send_sems.at[which, side],
                     recv_sems.at[which, 1 - side], device).wait_send()

    def parent_halo(side, do):
        halo(x_side, side, parent.at[0 if side == LOW else prows - 1],
             lambda where: prow.at[where], row_s, row_r, 0, do)
        halo(y_side, side, pcol_send.at[side], lambda where: pcol.at[where], col_s, col_r, 0, do)

    def nest_halo(turn, side, do, kinds=("x", "y")):
        if "x" in kinds:
            if turn == 0:
                src = nest.at[0 if side == LOW else nrows - 1]
            else:
                src = nrow_send.at[turn - 1, side]
            halo(x_side, side, src, lambda where: nrow.at[turn, where], row_s, row_r, 1 + turn, do)
        if "y" in kinds:
            halo(y_side, side, ncol_send.at[turn, side], lambda where: ncol.at[turn, where],
                 col_s, col_r, 1 + turn, do)

    def peer(k):
        return {"gx": lax.rem(me + k, n_x)}

    def key_copy(k):
        return copy(keys.at[0], keys.at[k], key_s.at[k], key_r.at[k], peer(k))

    def answer_copy(k):
        return copy(answers_send.at[k], answers.at[k], ans_s.at[k], ans_r.at[k],
                    {"gx": lax.rem(me + (n_x - k), n_x)})

    def mean_copy(k):
        return copy(means.at[0], means.at[k], mean_s.at[k], mean_r.at[k], peer(k))

    for side in (LOW, HIGH):
        parent_halo(side, "start")
    over(1, n_x, lambda k: key_copy(k).start())
    for side in (LOW, HIGH):
        nest_halo(0, side, "start")

    for r in range(prows):
        centre = parent[r].astype(F32)
        around = inside(centre, pcols)
        if r > 0:
            around = around + parent[r - 1].astype(F32)
        if r < prows - 1:
            around = around + parent[r + 1].astype(F32)
        stepped[r] = mix(centre + nu_parent_c * (around - 4.0 * centre))
    for side in (LOW, HIGH):
        parent_halo(side, "recv")
    row_low, row_high, col_low, col_high = from_halos(parent_lhs, prow, pcol)
    stepped[0] = stepped[0] + row_low
    stepped[prows - 1] = stepped[prows - 1] + row_high
    for r in range(prows):
        add_cols(stepped.at[r], r, pcols, col_low, col_high)
        stepped_bf[r * levels:(r + 1) * levels, :] = stepped[r].astype(BF16)

    parent_col = lax.broadcasted_iota(jnp.int32, (pcols, blocks), 0)
    shift = pcols.bit_length() - 1

    def row_of(k):
        return lax.shift_right_arithmetic(keys[k, 0:1, :] - me * (prows * pcols), shift)

    def places(k):
        return row_of(k), one_hot(parent_col == (keys[k, 0:1, :] & (pcols - 1)))

    parent_across = lax.broadcasted_iota(jnp.int32, (blocks, pcols), 1)

    def place_back(k):
        down = jnp.transpose(keys[k])[:, 0:1]
        back[k] = one_hot(parent_across == (down & (pcols - 1)))

    def serve(k):
        if not (isinstance(k, int) and k == 0):
            key_copy(k).wait_recv()
        row, hot = places(k)
        found = dot(stepped_bf[...], hot)
        total = jnp.zeros((levels, blocks), F32)
        for r in range(prows):
            total = jnp.where(row == r, found[r * levels:(r + 1) * levels], total)
        if isinstance(k, int) and k == 0:
            answers[0] = total.astype(BF16)
        else:
            answers_send[k] = total.astype(BF16)
            answer_copy(k).start()

    over(1, n_x, serve)
    serve(0)

    def weight(low_row):
        first = nest_of[lax.rem(low_row + total_rows, total_rows)]
        second = nest_of[lax.rem(low_row + 1, total_rows)]
        return jnp.where(first == second, 1.0, 0.0).astype(F32)

    weights = [weight(me * nrows + r - 1) for r in range(nrows + 1)]

    def diffuse(get, put):
        for r in range(nrows):
            centre = get(r)
            around = inside(centre, ncols)
            if r > 0:
                around = around + get(r - 1) * weights[r]
            if r < nrows - 1:
                around = around + get(r + 1) * weights[r + 1]
            put(r, mix(keep_c * (centre + nu_nest_c * (around - 4.0 * centre))))

    def nest_halos(turn):
        for side in (LOW, HIGH):
            nest_halo(turn, side, "recv")
        row_low, row_high, col_low, col_high = from_halos(nest_lhs, nrow.at[turn], ncol.at[turn])
        return row_low * weights[0], row_high * weights[nrows], col_low, col_high

    def put_state(r, value):
        state[0, r] = value

    diffuse(lambda r: nest[r].astype(F32), put_state)
    row_low, row_high, col_low, col_high = nest_halos(0)
    state[0, 0] = state[0, 0] + row_low
    state[0, nrows - 1] = state[0, nrows - 1] + row_high
    for r in range(nrows):
        add_cols(state.at[0, r], r, ncols, col_low, col_high)

    parent_row = lax.broadcasted_iota(jnp.int32, (16, blocks), 0)
    over(0, n_x, place_back)

    def count_step(k):
        return dot(one_hot(parent_row == row_of(k)), back[k])

    forced = answers[0].astype(F32)
    if n_x <= 8:
        counts = count_step(0)
        for k in range(1, n_x):
            counts = counts + count_step(k)
        for k in range(1, n_x):
            answer_copy(k).wait_recv()
            forced = forced + answers[k].astype(F32)
    else:
        counts = lax.fori_loop(
            0, n_x, lambda k, t: t + count_step(k), jnp.zeros((16, pcols), F32))

        def collect(k, t):
            answer_copy(k).wait_recv()
            return t + answers[k].astype(F32)

        forced = lax.fori_loop(1, n_x, collect, forced)

    block_at = lax.broadcasted_iota(jnp.int32, (bcols, ncols), 0)
    cell_at = lax.broadcasted_iota(jnp.int32, (bcols, ncols), 1)
    spread = one_hot((cell_at >= 3 * block_at) & (cell_at < 3 * block_at + 3))
    spread2 = jnp.concatenate([spread, spread], axis=0)
    drive = mix(relax_c * forced)
    for a in range(brows):
        high, low = split(drive[:, a * bcols:(a + 1) * bcols])
        pulled[a] = dot(jnp.concatenate([high, low], axis=1), spread2)

    def send_rows(turn, r, value):
        side = LOW if r == 0 else HIGH
        nrow_send[turn - 1, side] = value.astype(BF16)
        nest_halo(turn, side, "start", ("x",))

    for r in (0, nrows - 1, *range(1, nrows - 1)):
        value = state[0, r] + pulled[r // 3]
        state[0, r] = value
        if r in (0, nrows - 1):
            send_rows(1, r, value)
    for side, packed in enumerate(edges([state[0, r] for r in range(nrows)], ncols)):
        ncol_send[1, side] = packed.astype(BF16)
        nest_halo(1, side, "start", ("y",))

    for turn in range(1, TURNS):
        now, later = (turn - 1) % 2, turn % 2

        def put_next(r, value):
            state[later, r] = value + pulled[r // 3]

        diffuse(lambda r: state[now, r], put_next)
        ends = None
        if turn < TURNS - 1:
            ends = edges([state[later, r] for r in range(nrows)], ncols)
        row_low, row_high, col_low, col_high = nest_halos(turn)
        for r, added in ((0, row_low), (nrows - 1, row_high)):
            state[later, r] = state[later, r] + added
            add_cols(state.at[later, r], r, ncols, col_low, col_high)
            if turn < TURNS - 1:
                send_rows(turn + 1, r, state[later, r])
        if turn < TURNS - 1:
            for side, (end, at, own) in enumerate(
                zip(ends, (0, ncols - 1), (col_low, col_high))
            ):
                end = end + own
                end = end + jnp.where(lane128 == 0, row_low[:, at:at + 1], 0.0)
                end = end + jnp.where(lane128 == nrows - 1, row_high[:, at:at + 1], 0.0)
                ncol_send[turn + 1, side] = end.astype(BF16)
                nest_halo(turn + 1, side, "start", ("y",))
        for r in range(1, nrows - 1):
            add_cols(state.at[later, r], r, ncols, col_low, col_high)

    last = (TURNS - 1) % 2
    down_cell = lax.broadcasted_iota(jnp.int32, (ncols, bcols), 0)
    down_block = lax.broadcasted_iota(jnp.int32, (ncols, bcols), 1)
    gather_up = one_hot((down_cell >= 3 * down_block) & (down_cell < 3 * down_block + 3))
    for a in range(brows):
        summed = state[last, 3 * a] + state[last, 3 * a + 1] + state[last, 3 * a + 2]
        high, low = split(summed)
        both = dot(jnp.concatenate([high, low], axis=0), gather_up)
        mean = (both[:levels] + both[levels:]) * (1.0 / 9.0)
        means[0, :, a * bcols:(a + 1) * bcols] = mean.astype(BF16)
    over(1, n_x, lambda k: mean_copy(k).start())
    for r in range(nrows):
        nest_out[r] = state[last, r].astype(BF16)
    store_nest = pltpu.make_async_copy(nest_out, nest_out_h, out_sem)
    store_nest.start()

    def give(k, total):
        row = row_of(k)
        mean = means[k].astype(F32)
        shared = jnp.concatenate(
            [jnp.where(row == r, mean, 0.0).astype(BF16) for r in range(prows)], axis=0
        )
        return total + dot(shared, back[k])

    for r in range(prows):
        stepped[r] = stepped[r] * (1.0 - feedback_c * counts[r:r + 1, :])
    returned = give(0, jnp.zeros((prows * levels, pcols), F32))
    if n_x <= 8:
        for k in range(1, n_x):
            mean_copy(k).wait_recv()
            returned = give(k, returned)
    else:
        def give_next(k, total):
            mean_copy(k).wait_recv()
            return give(k, total)

        returned = lax.fori_loop(1, n_x, give_next, returned)
    for r in range(prows):
        given = returned[r * levels:(r + 1) * levels]
        parent_out[r] = (stepped[r] + feedback_c * given).astype(BF16)

    for side in (LOW, HIGH):
        parent_halo(side, "send")
        for turn in range(TURNS):
            nest_halo(turn, side, "send")

    def sent(k):
        key_copy(k).wait_send()
        answer_copy(k).wait_send()
        mean_copy(k).wait_send()

    over(1, n_x, sent)
    store_nest.wait()


def body(n_x, n_gy, n_gz, parent, nest, nu_p, nu_n, relax, feedback, vert_mix, owner, cell, nest_of):
    levels, prows, pcols = parent.shape
    _, nrows, ncols = nest.shape
    blocks = cell.size
    vmem = pl.BlockSpec(memory_space=pltpu.VMEM)
    dma = pltpu.SemaphoreType.DMA
    parent_out, nest_out = pl.pallas_call(
        functools.partial(kernel, n_x, n_gy, n_gz),
        out_shape=(
            jax.ShapeDtypeStruct((prows, levels, pcols), BF16),
            jax.ShapeDtypeStruct((nrows, levels, ncols), BF16),
        ),
        in_specs=[pl.BlockSpec(memory_space=pltpu.HBM)] * 10,
        out_specs=(vmem, pl.BlockSpec(memory_space=pltpu.HBM)),
        scratch_shapes=[
            pltpu.VMEM(parent.shape, BF16),
            pltpu.VMEM((nrows, levels, ncols), BF16),
            *[pltpu.VMEM((1, levels), F32)] * 4,
            pltpu.VMEM((levels, levels), F32),
            *[pltpu.VMEM((1, blocks), jnp.int32)] * 2,
            pltpu.SMEM(nest_of.shape, jnp.int32),
            pltpu.VMEM((pcols // 128, levels * prows, 128), F32),
            pltpu.VMEM((prows, levels, pcols), BF16),
            dma((10,)),
            pltpu.VMEM((nrows, levels, ncols), BF16),
            dma,
            pltpu.VMEM((n_x, 8, blocks), jnp.int32),
            pltpu.VMEM((2, levels, pcols), BF16),
            pltpu.VMEM((2, levels, 128), BF16),
            pltpu.VMEM((2, levels, 128), BF16),
            pltpu.VMEM((TURNS, 2, levels, ncols), BF16),
            pltpu.VMEM((TURNS - 1, 2, levels, ncols), BF16),
            pltpu.VMEM((TURNS, 2, levels, 128), BF16),
            pltpu.VMEM((TURNS, 2, levels, 128), BF16),
            pltpu.VMEM((2, nrows, levels, ncols), F32),
            pltpu.VMEM((prows, levels, pcols), F32),
            pltpu.VMEM((prows * levels, pcols), BF16),
            pltpu.VMEM((n_x, levels, blocks), BF16),
            pltpu.VMEM((n_x, levels, blocks), BF16),
            pltpu.VMEM((n_x, levels, blocks), BF16),
            pltpu.VMEM((levels, 3 * levels), BF16),
            pltpu.VMEM((nrows // 3, levels, ncols), F32),
            pltpu.VMEM((n_x, blocks, pcols), BF16),
            dma((1 + TURNS, 2)), dma((1 + TURNS, 2)), dma((1 + TURNS, 2)), dma((1 + TURNS, 2)),
            dma((n_x,)), dma((n_x,)), dma((n_x,)), dma((n_x,)), dma((n_x,)), dma((n_x,)),
        ],
        compiler_params=pltpu.CompilerParams(
            collective_id=0, has_side_effects=True, vmem_limit_bytes=62 * 1024 * 1024
        ),
    )(
        parent, nest.transpose(1, 0, 2),
        nu_p.reshape(1, -1), nu_n.reshape(1, -1), relax.reshape(1, -1), feedback.reshape(1, -1),
        vert_mix, owner.reshape(1, -1), cell.reshape(1, -1), nest_of,
    )
    return parent_out.transpose(1, 0, 2), nest_out.transpose(1, 0, 2)


def solution(mesh):
    sizes = mesh.shape
    grid = P("groups", "gx", ("gy", "gz"))
    placed = (
        grid, grid, P(), P(), P(), P(), P(),
        P("gx", ("gy", "gz"), None, None), P("gx", ("gy", "gz"), None), P(),
    )
    return jax.shard_map(
        functools.partial(body, sizes["gx"], sizes["gy"], sizes["gz"]),
        mesh=mesh,
        in_specs=placed,
        out_specs=(grid, grid),
        check_vma=False,
    )
```

```python
import functools

import jax
import jax.numpy as jnp
from jax import lax
from jax.experimental import pallas as pl
from jax.experimental.pallas import tpu as pltpu
from jax.sharding import PartitionSpec as P

MESH = pl.DeviceIdType.MESH
F32 = jnp.float32
BF16 = jnp.bfloat16
LOW, HIGH = 0, 1
TURNS = 3


def dot(a, b):
    return jnp.dot(a, b, preferred_element_type=F32)


def one_hot(mask):
    return jnp.where(mask, 1.0, 0.0).astype(BF16)


def split(x):
    high = x.astype(BF16)
    return high, (x - high.astype(F32)).astype(BF16)


def over(first, count, step):
    if count <= 8:
        for k in range(first, count):
            step(k)
    else:
        lax.fori_loop(first, count, lambda k, _: (step(k), 0)[1], 0)


def kernel(
    n_x, n_gy, n_gz,
    parent_h, nest_h, nu_p_h, nu_n_h, relax_h, feedback_h, vert_mix_h, owner_h, cell_h, nest_of_h,
    parent_out, nest_out_h,
    parent_n, nest, nu_p, nu_n, relax, feedback, vert_mix, owner, cell, nest_of, turned, parent,
    in_sem, nest_out, out_sem,
    keys, prow, pcol, pcol_send, nrow, nrow_send, ncol, ncol_send,
    state, stepped, stepped_bf, answers, answers_send, means, lhs, pulled, back,
    row_s, row_r, col_s, col_r, key_s, key_r, ans_s, ans_r, mean_s, mean_r,
):
    loads = [
        pltpu.make_async_copy(src, dst, in_sem.at[i])
        for i, (src, dst) in enumerate((
            (parent_h, parent_n), (nest_h, nest), (owner_h, owner), (cell_h, cell),
            (vert_mix_h, vert_mix), (nu_p_h, nu_p), (nu_n_h, nu_n), (relax_h, relax),
            (feedback_h, feedback), (nest_of_h, nest_of),
        ))
    ]
    for load in loads:
        load.start()
    prows, levels, pcols = parent.shape
    nrows, _, ncols = nest.shape
    brows, bcols = nrows // 3, ncols // 3
    blocks = brows * bcols
    total_rows = nest_of.shape[0]
    me = lax.axis_index("gx")
    tile = lax.axis_index("gy") * n_gz + lax.axis_index("gz")
    n_y = n_gy * n_gz

    def y_device(t):
        return {"gy": t // n_gz, "gz": t % n_gz}

    x_side = ((me > 0, {"gx": me - 1}), (me < n_x - 1, {"gx": me + 1}))
    y_side = ((tile > 0, y_device(tile - 1)), (tile < n_y - 1, y_device(tile + 1)))

    barrier = pltpu.get_barrier_semaphore()

    def greet(k):
        pl.semaphore_signal(
            barrier, inc=1, device_id={"gx": lax.rem(me + k, n_x)}, device_id_type=MESH
        )

    over(1, n_x, greet)
    for present, device in y_side:
        @pl.when(present)
        def _():
            pl.semaphore_signal(barrier, inc=1, device_id=device, device_id_type=MESH)

    lane128 = lax.broadcasted_iota(jnp.int32, (levels, 128), 1)

    def pack(columns):
        packed = jnp.zeros((levels, 128), F32)
        for r, column in enumerate(columns):
            packed = jnp.where(lane128 == r, column, packed)
        return packed

    def edges(rows, width):
        low = pack([rows[r][:, 0:1] for r in range(len(rows))])
        high = pack([rows[r][:, width - 1:width] for r in range(len(rows))])
        return low, high

    for load in loads:
        load.wait()
    whole = parent_n[...].astype(F32)
    p = []
    for h in range(pcols // 128):
        turned[h] = whole[:, :, h * 128:(h + 1) * 128].reshape(levels * prows, 128)
    for r in range(prows):
        row = jnp.concatenate(
            [turned[h, pl.ds(r, levels, stride=prows), :] for h in range(pcols // 128)], axis=1
        )
        parent[r] = row.astype(BF16)
        p.append(row)
    for side, packed in enumerate(edges(p, pcols)):
        pcol_send[side] = packed.astype(BF16)
    s = [nest[r].astype(F32) for r in range(nrows)]
    for side, packed in enumerate(edges(s, ncols)):
        ncol_send[0, side] = packed.astype(BF16)
    key = owner[...] * (prows * pcols) + cell[...]
    keys[0] = jnp.broadcast_to(key, keys.shape[1:])

    for side in (LOW, HIGH):
        @pl.when(jnp.logical_not(x_side[side][0]))
        def _():
            prow[side] = jnp.zeros(prow.shape[1:], BF16)
            for turn in range(TURNS):
                nrow[turn, side] = jnp.zeros(nrow.shape[2:], BF16)

        @pl.when(jnp.logical_not(y_side[side][0]))
        def _():
            pcol[side] = jnp.zeros(pcol.shape[1:], BF16)
            for turn in range(TURNS):
                ncol[turn, side] = jnp.zeros(ncol.shape[2:], BF16)

    def level_column(ref):
        at = lax.broadcasted_iota(jnp.int32, (levels, levels), 0)
        across = lax.broadcasted_iota(jnp.int32, (levels, levels), 1)
        return jnp.sum(jnp.where(at == across, ref[...], 0.0), axis=1, keepdims=True)

    nu_parent_c, nu_nest_c = level_column(nu_p), level_column(nu_n)
    relax_c, feedback_c = level_column(relax), level_column(feedback)
    keep_c = 1.0 - relax_c

    m_high, m_low = split(vert_mix[...])
    wide_at = lax.broadcasted_iota(jnp.int32, (levels, 3 * levels), 0)
    wide_across = lax.broadcasted_iota(jnp.int32, (levels, 3 * levels), 1)
    place_high = one_hot((wide_across == wide_at) | (wide_across == wide_at + levels))
    place_low = one_hot(wide_across == wide_at + 2 * levels)
    lhs[...] = (dot(m_high, place_high) + dot(m_low, place_low)).astype(BF16)

    def mix(x):
        high, low = split(x)
        return dot(lhs[...], jnp.concatenate([high, low, high], axis=0))

    def inside(x, width):
        lane = lax.broadcasted_iota(jnp.int32, (levels, width), 1)
        before = jnp.where(lane == 0, 0.0, pltpu.roll(x, 1, axis=1))
        after = jnp.where(lane == width - 1, 0.0, pltpu.roll(x, width - 1, axis=1))
        return before + after

    def halo_matrix(scale):
        high, low = split(vert_mix[...] * scale)
        at = lax.broadcasted_iota(jnp.int32, (levels, 2 * levels), 0)
        across = lax.broadcasted_iota(jnp.int32, (levels, 2 * levels), 1)
        return (
            dot(high, one_hot(across == at)) + dot(low, one_hot(across == at + levels))
        ).astype(BF16)

    parent_lhs = halo_matrix(nu_p[...])
    nest_lhs = halo_matrix(nu_n[...] * (1.0 - relax[...]))

    def from_halos(matrix, rows, cols):
        halos = jnp.concatenate([rows[LOW], rows[HIGH], cols[LOW], cols[HIGH]], axis=1)
        added = dot(matrix, jnp.concatenate([halos, halos], axis=0))
        width = rows.shape[-1]
        return (
            added[:, :width], added[:, width:2 * width],
            added[:, 2 * width:2 * width + 128], added[:, 2 * width + 128:],
        )

    def add_cols(target, r, width, low, high):
        target[:, :128] = target[:, :128] + jnp.where(lane128 == 0, low[:, r:r + 1], 0.0)
        target[:, width - 128:] = target[:, width - 128:] + jnp.where(
            lane128 == 127, high[:, r:r + 1], 0.0)

    callers = n_x - 1 + sum(present.astype(jnp.int32) for present, _ in y_side)
    pl.semaphore_wait(barrier, callers)

    def copy(src, dst, send_sem, recv_sem, device):
        return pltpu.make_async_remote_copy(
            src_ref=src, dst_ref=dst, send_sem=send_sem, recv_sem=recv_sem,
            device_id=device, device_id_type=MESH,
        )

    def halo(sides, side, src, dst, send_sems, recv_sems, which, do):
        present, device = sides[side]

        @pl.when(present)
        def _():
            if do == "start":
                copy(src, dst(1 - side), send_sems.at[which, side],
                     recv_sems.at[which, 1 - side], device).start()
            elif do == "recv":
                copy(src, dst(side), send_sems.at[which, side],
                     recv_sems.at[which, side], device).wait_recv()
            else:
                copy(src, dst(1 - side), send_sems.at[which, side],
                     recv_sems.at[which, 1 - side], device).wait_send()

    def parent_halo(side, do):
        halo(x_side, side, parent.at[0 if side == LOW else prows - 1],
             lambda where: prow.at[where], row_s, row_r, 0, do)
        halo(y_side, side, pcol_send.at[side], lambda where: pcol.at[where], col_s, col_r, 0, do)

    def nest_halo(turn, side, do, kinds=("x", "y")):
        if "x" in kinds:
            if turn == 0:
                src = nest.at[0 if side == LOW else nrows - 1]
            else:
                src = nrow_send.at[turn - 1, side]
            halo(x_side, side, src, lambda where: nrow.at[turn, where], row_s, row_r, 1 + turn, do)
        if "y" in kinds:
            halo(y_side, side, ncol_send.at[turn, side], lambda where: ncol.at[turn, where],
                 col_s, col_r, 1 + turn, do)

    def peer(k):
        return {"gx": lax.rem(me + k, n_x)}

    def key_copy(k):
        return copy(keys.at[0], keys.at[k], key_s.at[k], key_r.at[k], peer(k))

    def answer_copy(k):
        return copy(answers_send.at[k], answers.at[k], ans_s.at[k], ans_r.at[k],
                    {"gx": lax.rem(me + (n_x - k), n_x)})

    def mean_copy(k):
        return copy(means.at[0], means.at[k], mean_s.at[k], mean_r.at[k], peer(k))

    for side in (LOW, HIGH):
        parent_halo(side, "start")
    over(1, n_x, lambda k: key_copy(k).start())
    for side in (LOW, HIGH):
        nest_halo(0, side, "start")

    for r in range(prows):
        centre = parent[r].astype(F32)
        around = inside(centre, pcols)
        if r > 0:
            around = around + parent[r - 1].astype(F32)
        if r < prows - 1:
            around = around + parent[r + 1].astype(F32)
        stepped[r] = mix(centre + nu_parent_c * (around - 4.0 * centre))
    for side in (LOW, HIGH):
        parent_halo(side, "recv")
    row_low, row_high, col_low, col_high = from_halos(parent_lhs, prow, pcol)
    stepped[0] = stepped[0] + row_low
    stepped[prows - 1] = stepped[prows - 1] + row_high
    for r in range(prows):
        add_cols(stepped.at[r], r, pcols, col_low, col_high)
        stepped_bf[r * levels:(r + 1) * levels, :] = stepped[r].astype(BF16)

    parent_col = lax.broadcasted_iota(jnp.int32, (pcols, blocks), 0)
    shift = pcols.bit_length() - 1

    def row_of(k):
        return lax.shift_right_arithmetic(keys[k, 0:1, :] - me * (prows * pcols), shift)

    def places(k):
        return row_of(k), one_hot(parent_col == (keys[k, 0:1, :] & (pcols - 1)))

    parent_across = lax.broadcasted_iota(jnp.int32, (blocks, pcols), 1)

    def place_back(k):
        down = jnp.transpose(keys[k])[:, 0:1]
        back[k] = one_hot(parent_across == (down & (pcols - 1)))

    def serve(k):
        if not (isinstance(k, int) and k == 0):
            key_copy(k).wait_recv()
        row, hot = places(k)
        found = dot(stepped_bf[...], hot)
        total = jnp.zeros((levels, blocks), F32)
        for r in range(prows):
            total = jnp.where(row == r, found[r * levels:(r + 1) * levels], total)
        if isinstance(k, int) and k == 0:
            answers[0] = total.astype(BF16)
        else:
            answers_send[k] = total.astype(BF16)
            answer_copy(k).start()

    over(1, n_x, serve)
    serve(0)

    def weight(low_row):
        first = nest_of[lax.rem(low_row + total_rows, total_rows)]
        second = nest_of[lax.rem(low_row + 1, total_rows)]
        return jnp.where(first == second, 1.0, 0.0).astype(F32)

    weights = [weight(me * nrows + r - 1) for r in range(nrows + 1)]

    def diffuse(get, put):
        for r in range(nrows):
            centre = get(r)
            around = inside(centre, ncols)
            if r > 0:
                around = around + get(r - 1) * weights[r]
            if r < nrows - 1:
                around = around + get(r + 1) * weights[r + 1]
            put(r, mix(keep_c * (centre + nu_nest_c * (around - 4.0 * centre))))

    def nest_halos(turn):
        for side in (LOW, HIGH):
            nest_halo(turn, side, "recv")
        row_low, row_high, col_low, col_high = from_halos(nest_lhs, nrow.at[turn], ncol.at[turn])
        return row_low * weights[0], row_high * weights[nrows], col_low, col_high

    def put_state(r, value):
        state[0, r] = value

    diffuse(lambda r: nest[r].astype(F32), put_state)
    row_low, row_high, col_low, col_high = nest_halos(0)
    state[0, 0] = state[0, 0] + row_low
    state[0, nrows - 1] = state[0, nrows - 1] + row_high
    for r in range(nrows):
        add_cols(state.at[0, r], r, ncols, col_low, col_high)

    parent_row = lax.broadcasted_iota(jnp.int32, (16, blocks), 0)
    over(0, n_x, place_back)

    def count_step(k):
        return dot(one_hot(parent_row == row_of(k)), back[k])

    forced = answers[0].astype(F32)
    if n_x <= 8:
        counts = count_step(0)
        for k in range(1, n_x):
            counts = counts + count_step(k)
        for k in range(1, n_x):
            answer_copy(k).wait_recv()
            forced = forced + answers[k].astype(F32)
    else:
        counts = lax.fori_loop(
            0, n_x, lambda k, t: t + count_step(k), jnp.zeros((16, pcols), F32))

        def collect(k, t):
            answer_copy(k).wait_recv()
            return t + answers[k].astype(F32)

        forced = lax.fori_loop(1, n_x, collect, forced)

    block_at = lax.broadcasted_iota(jnp.int32, (bcols, ncols), 0)
    cell_at = lax.broadcasted_iota(jnp.int32, (bcols, ncols), 1)
    spread = one_hot((cell_at >= 3 * block_at) & (cell_at < 3 * block_at + 3))
    spread2 = jnp.concatenate([spread, spread], axis=0)
    drive = mix(relax_c * forced)
    for a in range(brows):
        high, low = split(drive[:, a * bcols:(a + 1) * bcols])
        pulled[a] = dot(jnp.concatenate([high, low], axis=1), spread2)

    def send_rows(turn, r, value):
        side = LOW if r == 0 else HIGH
        nrow_send[turn - 1, side] = value.astype(BF16)
        nest_halo(turn, side, "start", ("x",))

    for r in (0, nrows - 1, *range(1, nrows - 1)):
        value = state[0, r] + pulled[r // 3]
        state[0, r] = value
        if r in (0, nrows - 1):
            send_rows(1, r, value)
    for side, packed in enumerate(edges([state[0, r] for r in range(nrows)], ncols)):
        ncol_send[1, side] = packed.astype(BF16)
        nest_halo(1, side, "start", ("y",))

    for turn in range(1, TURNS):
        now, later = (turn - 1) % 2, turn % 2

        def put_next(r, value):
            state[later, r] = value + pulled[r // 3]

        diffuse(lambda r: state[now, r], put_next)
        ends = None
        if turn < TURNS - 1:
            ends = edges([state[later, r] for r in range(nrows)], ncols)
        row_low, row_high, col_low, col_high = nest_halos(turn)
        for r, added in ((0, row_low), (nrows - 1, row_high)):
            state[later, r] = state[later, r] + added
            add_cols(state.at[later, r], r, ncols, col_low, col_high)
            if turn < TURNS - 1:
                send_rows(turn + 1, r, state[later, r])
        if turn < TURNS - 1:
            for side, (end, at, own) in enumerate(
                zip(ends, (0, ncols - 1), (col_low, col_high))
            ):
                end = end + own
                end = end + jnp.where(lane128 == 0, row_low[:, at:at + 1], 0.0)
                end = end + jnp.where(lane128 == nrows - 1, row_high[:, at:at + 1], 0.0)
                ncol_send[turn + 1, side] = end.astype(BF16)
                nest_halo(turn + 1, side, "start", ("y",))
        for r in range(1, nrows - 1):
            add_cols(state.at[later, r], r, ncols, col_low, col_high)

    last = (TURNS - 1) % 2
    down_cell = lax.broadcasted_iota(jnp.int32, (ncols, bcols), 0)
    down_block = lax.broadcasted_iota(jnp.int32, (ncols, bcols), 1)
    gather_up = one_hot((down_cell >= 3 * down_block) & (down_cell < 3 * down_block + 3))
    for a in range(brows):
        summed = state[last, 3 * a] + state[last, 3 * a + 1] + state[last, 3 * a + 2]
        high, low = split(summed)
        both = dot(jnp.concatenate([high, low], axis=0), gather_up)
        mean = (both[:levels] + both[levels:]) * (1.0 / 9.0)
        means[0, :, a * bcols:(a + 1) * bcols] = mean.astype(BF16)
    over(1, n_x, lambda k: mean_copy(k).start())
    for r in range(nrows):
        nest_out[r] = state[last, r].astype(BF16)
    store_nest = pltpu.make_async_copy(nest_out, nest_out_h, out_sem)
    store_nest.start()

    def give(k, total):
        row = row_of(k)
        mean = means[k].astype(F32)
        shared = jnp.concatenate(
            [jnp.where(row == r, mean, 0.0).astype(BF16) for r in range(prows)], axis=0
        )
        return total + dot(shared, back[k])

    for r in range(prows):
        stepped[r] = stepped[r] * (1.0 - feedback_c * counts[r:r + 1, :])
    returned = give(0, jnp.zeros((prows * levels, pcols), F32))
    if n_x <= 8:
        for k in range(1, n_x):
            mean_copy(k).wait_recv()
            returned = give(k, returned)
    else:
        def give_next(k, total):
            mean_copy(k).wait_recv()
            return give(k, total)

        returned = lax.fori_loop(1, n_x, give_next, returned)
    for r in range(prows):
        given = returned[r * levels:(r + 1) * levels]
        whole_row = stepped[r] + feedback_c * given
        for h in range(pcols // 128):
            turned[h, pl.ds(r, levels, stride=prows), :] = whole_row[:, h * 128:(h + 1) * 128]
    for h in range(pcols // 128):
        parent_out[:, :, h * 128:(h + 1) * 128] = turned[h].reshape(
            levels, prows, 128).astype(BF16)

    for side in (LOW, HIGH):
        parent_halo(side, "send")
        for turn in range(TURNS):
            nest_halo(turn, side, "send")

    def sent(k):
        key_copy(k).wait_send()
        answer_copy(k).wait_send()
        mean_copy(k).wait_send()

    over(1, n_x, sent)
    store_nest.wait()


def hand_over(parent, nest, parent_out, nest_out, parent_sem, nest_sem):
    first = pltpu.make_async_copy(parent, parent_out, parent_sem)
    second = pltpu.make_async_copy(nest, nest_out, nest_sem)
    first.start()
    second.start()
    first.wait()
    second.wait()


def body(n_x, n_gy, n_gz, parent, nest, nu_p, nu_n, relax, feedback, vert_mix, owner, cell, nest_of):
    levels, prows, pcols = parent.shape
    _, nrows, ncols = nest.shape
    blocks = cell.size
    vmem = pl.BlockSpec(memory_space=pltpu.VMEM)
    dma = pltpu.SemaphoreType.DMA
    parent_out, nest_out = pl.pallas_call(
        functools.partial(kernel, n_x, n_gy, n_gz),
        out_shape=(
            jax.ShapeDtypeStruct((levels, prows, pcols), BF16),
            jax.ShapeDtypeStruct((nrows, levels, ncols), BF16),
        ),
        in_specs=[pl.BlockSpec(memory_space=pltpu.HBM)] * 10,
        out_specs=(vmem, pl.BlockSpec(memory_space=pltpu.HBM)),
        scratch_shapes=[
            pltpu.VMEM(parent.shape, BF16),
            pltpu.VMEM((nrows, levels, ncols), BF16),
            *[pltpu.VMEM((1, levels), F32)] * 4,
            pltpu.VMEM((levels, levels), F32),
            *[pltpu.VMEM((1, blocks), jnp.int32)] * 2,
            pltpu.SMEM(nest_of.shape, jnp.int32),
            pltpu.VMEM((pcols // 128, levels * prows, 128), F32),
            pltpu.VMEM((prows, levels, pcols), BF16),
            dma((10,)),
            pltpu.VMEM((nrows, levels, ncols), BF16),
            dma,
            pltpu.VMEM((n_x, 8, blocks), jnp.int32),
            pltpu.VMEM((2, levels, pcols), BF16),
            pltpu.VMEM((2, levels, 128), BF16),
            pltpu.VMEM((2, levels, 128), BF16),
            pltpu.VMEM((TURNS, 2, levels, ncols), BF16),
            pltpu.VMEM((TURNS - 1, 2, levels, ncols), BF16),
            pltpu.VMEM((TURNS, 2, levels, 128), BF16),
            pltpu.VMEM((TURNS, 2, levels, 128), BF16),
            pltpu.VMEM((2, nrows, levels, ncols), F32),
            pltpu.VMEM((prows, levels, pcols), F32),
            pltpu.VMEM((prows * levels, pcols), BF16),
            pltpu.VMEM((n_x, levels, blocks), BF16),
            pltpu.VMEM((n_x, levels, blocks), BF16),
            pltpu.VMEM((n_x, levels, blocks), BF16),
            pltpu.VMEM((levels, 3 * levels), BF16),
            pltpu.VMEM((nrows // 3, levels, ncols), F32),
            pltpu.VMEM((n_x, blocks, pcols), BF16),
            dma((1 + TURNS, 2)), dma((1 + TURNS, 2)), dma((1 + TURNS, 2)), dma((1 + TURNS, 2)),
            dma((n_x,)), dma((n_x,)), dma((n_x,)), dma((n_x,)), dma((n_x,)), dma((n_x,)),
        ],
        compiler_params=pltpu.CompilerParams(
            collective_id=0, has_side_effects=True, vmem_limit_bytes=62 * 1024 * 1024
        ),
    )(
        parent, nest.transpose(1, 0, 2),
        nu_p.reshape(1, -1), nu_n.reshape(1, -1), relax.reshape(1, -1), feedback.reshape(1, -1),
        vert_mix, owner.reshape(1, -1), cell.reshape(1, -1), nest_of,
    )
    hbm = pl.BlockSpec(memory_space=pltpu.HBM)
    parent_out, nest_out = pl.pallas_call(
        hand_over,
        out_shape=(
            jax.ShapeDtypeStruct(parent_out.shape, BF16),
            jax.ShapeDtypeStruct(nest_out.shape, BF16),
        ),
        in_specs=[hbm, hbm],
        out_specs=(hbm, hbm),
        scratch_shapes=[dma, dma],
        compiler_params=pltpu.CompilerParams(vmem_limit_bytes=62 * 1024 * 1024),
    )(parent_out, nest_out)
    return parent_out, nest_out.transpose(1, 0, 2)


def solution(mesh):
    sizes = mesh.shape
    grid = P("groups", "gx", ("gy", "gz"))
    placed = (
        grid, grid, P(), P(), P(), P(), P(),
        P("gx", ("gy", "gz"), None, None), P("gx", ("gy", "gz"), None), P(),
    )
    return jax.shard_map(
        functools.partial(body, sizes["gx"], sizes["gy"], sizes["gz"]),
        mesh=mesh,
        in_specs=placed,
        out_specs=(grid, grid),
        check_vma=False,
    )
```

```python
import functools

import jax
import jax.numpy as jnp
from jax import lax
from jax.experimental import pallas as pl
from jax.experimental.pallas import tpu as pltpu
from jax.sharding import PartitionSpec as P

MESH = pl.DeviceIdType.MESH
F32 = jnp.float32
BF16 = jnp.bfloat16
LOW, HIGH = 0, 1
TURNS = 3


def dot(a, b):
    return jnp.dot(a, b, preferred_element_type=F32)


def one_hot(mask):
    return jnp.where(mask, 1.0, 0.0).astype(BF16)


def split(x):
    high = x.astype(BF16)
    return high, (x - high.astype(F32)).astype(BF16)


def over(first, count, step):
    if count <= 8:
        for k in range(first, count):
            step(k)
    else:
        lax.fori_loop(first, count, lambda k, _: (step(k), 0)[1], 0)


def kernel(
    n_x, n_gy, n_gz,
    parent_h, nest_h, nu_p_h, nu_n_h, relax_h, feedback_h, vert_mix_h, owner_h, cell_h, nest_of_h,
    parent_out, nest_out_h,
    parent_n, nest, nu_p, nu_n, relax, feedback, vert_mix, owner, cell, nest_of, turned, parent,
    in_sem, nest_out, out_sem,
    keys, prow, pcol, pcol_send, nrow, nrow_send, ncol, ncol_send,
    state, stepped, stepped_bf, answers, answers_send, means, lhs, pulled, back,
    row_s, row_r, col_s, col_r, key_s, key_r, ans_s, ans_r, mean_s, mean_r,
):
    loads = [
        pltpu.make_async_copy(src, dst, in_sem.at[i])
        for i, (src, dst) in enumerate((
            (parent_h, parent_n), (nest_h, nest), (owner_h, owner), (cell_h, cell),
            (vert_mix_h, vert_mix), (nu_p_h, nu_p), (nu_n_h, nu_n), (relax_h, relax),
            (feedback_h, feedback), (nest_of_h, nest_of),
        ))
    ]
    for load in loads:
        load.start()
    prows, levels, pcols = parent.shape
    nrows, _, ncols = nest.shape
    brows, bcols = nrows // 3, ncols // 3
    blocks = brows * bcols
    total_rows = nest_of.shape[0]
    me = lax.axis_index("gx")
    tile = lax.axis_index("gy") * n_gz + lax.axis_index("gz")
    n_y = n_gy * n_gz

    def y_device(t):
        return {"gy": t // n_gz, "gz": t % n_gz}

    x_side = ((me > 0, {"gx": me - 1}), (me < n_x - 1, {"gx": me + 1}))
    y_side = ((tile > 0, y_device(tile - 1)), (tile < n_y - 1, y_device(tile + 1)))

    barrier = pltpu.get_barrier_semaphore()

    def greet(k):
        pl.semaphore_signal(
            barrier, inc=1, device_id={"gx": lax.rem(me + k, n_x)}, device_id_type=MESH
        )

    over(1, n_x, greet)
    for present, device in y_side:
        @pl.when(present)
        def _():
            pl.semaphore_signal(barrier, inc=1, device_id=device, device_id_type=MESH)

    lane128 = lax.broadcasted_iota(jnp.int32, (levels, 128), 1)

    def pack(columns):
        packed = jnp.zeros((levels, 128), F32)
        for r, column in enumerate(columns):
            packed = jnp.where(lane128 == r, column, packed)
        return packed

    def edges(rows, width):
        low = pack([rows[r][:, 0:1] for r in range(len(rows))])
        high = pack([rows[r][:, width - 1:width] for r in range(len(rows))])
        return low, high

    for load in loads:
        load.wait()
    whole = parent_n[...].astype(F32)
    p = []
    for h in range(pcols // 128):
        turned[h] = whole[:, :, h * 128:(h + 1) * 128].reshape(levels * prows, 128)
    for r in range(prows):
        row = jnp.concatenate(
            [turned[h, pl.ds(r, levels, stride=prows), :] for h in range(pcols // 128)], axis=1
        )
        parent[r] = row.astype(BF16)
        p.append(row)
    for side, packed in enumerate(edges(p, pcols)):
        pcol_send[side] = packed.astype(BF16)
    s = [nest[r].astype(F32) for r in range(nrows)]
    for side, packed in enumerate(edges(s, ncols)):
        ncol_send[0, side] = packed.astype(BF16)
    key = owner[...] * (prows * pcols) + cell[...]
    keys[0] = jnp.broadcast_to(key, keys.shape[1:])

    for side in (LOW, HIGH):
        @pl.when(jnp.logical_not(x_side[side][0]))
        def _():
            prow[side] = jnp.zeros(prow.shape[1:], BF16)
            for turn in range(TURNS):
                nrow[turn, side] = jnp.zeros(nrow.shape[2:], BF16)

        @pl.when(jnp.logical_not(y_side[side][0]))
        def _():
            pcol[side] = jnp.zeros(pcol.shape[1:], BF16)
            for turn in range(TURNS):
                ncol[turn, side] = jnp.zeros(ncol.shape[2:], BF16)

    def level_column(ref):
        at = lax.broadcasted_iota(jnp.int32, (levels, levels), 0)
        across = lax.broadcasted_iota(jnp.int32, (levels, levels), 1)
        return jnp.sum(jnp.where(at == across, ref[...], 0.0), axis=1, keepdims=True)

    nu_parent_c, nu_nest_c = level_column(nu_p), level_column(nu_n)
    relax_c, feedback_c = level_column(relax), level_column(feedback)
    keep_c = 1.0 - relax_c

    m_high, m_low = split(vert_mix[...])
    wide_at = lax.broadcasted_iota(jnp.int32, (levels, 3 * levels), 0)
    wide_across = lax.broadcasted_iota(jnp.int32, (levels, 3 * levels), 1)
    place_high = one_hot((wide_across == wide_at) | (wide_across == wide_at + levels))
    place_low = one_hot(wide_across == wide_at + 2 * levels)
    lhs[...] = (dot(m_high, place_high) + dot(m_low, place_low)).astype(BF16)

    def mix(x):
        high, low = split(x)
        return dot(lhs[...], jnp.concatenate([high, low, high], axis=0))

    def inside(x, width):
        lane = lax.broadcasted_iota(jnp.int32, (levels, width), 1)
        before = jnp.where(lane == 0, 0.0, pltpu.roll(x, 1, axis=1))
        after = jnp.where(lane == width - 1, 0.0, pltpu.roll(x, width - 1, axis=1))
        return before + after

    def halo_matrix(scale):
        high, low = split(vert_mix[...] * scale)
        at = lax.broadcasted_iota(jnp.int32, (levels, 2 * levels), 0)
        across = lax.broadcasted_iota(jnp.int32, (levels, 2 * levels), 1)
        return (
            dot(high, one_hot(across == at)) + dot(low, one_hot(across == at + levels))
        ).astype(BF16)

    parent_lhs = halo_matrix(nu_p[...])
    nest_lhs = halo_matrix(nu_n[...] * (1.0 - relax[...]))

    def from_halos(matrix, rows, cols):
        halos = jnp.concatenate([rows[LOW], rows[HIGH], cols[LOW], cols[HIGH]], axis=1)
        added = dot(matrix, jnp.concatenate([halos, halos], axis=0))
        width = rows.shape[-1]
        return (
            added[:, :width], added[:, width:2 * width],
            added[:, 2 * width:2 * width + 128], added[:, 2 * width + 128:],
        )

    def add_cols(target, r, width, low, high):
        target[:, :128] = target[:, :128] + jnp.where(lane128 == 0, low[:, r:r + 1], 0.0)
        target[:, width - 128:] = target[:, width - 128:] + jnp.where(
            lane128 == 127, high[:, r:r + 1], 0.0)

    callers = n_x - 1 + sum(present.astype(jnp.int32) for present, _ in y_side)
    pl.semaphore_wait(barrier, callers)

    def copy(src, dst, send_sem, recv_sem, device):
        return pltpu.make_async_remote_copy(
            src_ref=src, dst_ref=dst, send_sem=send_sem, recv_sem=recv_sem,
            device_id=device, device_id_type=MESH,
        )

    def halo(sides, side, src, dst, send_sems, recv_sems, which, do):
        present, device = sides[side]

        @pl.when(present)
        def _():
            if do == "start":
                copy(src, dst(1 - side), send_sems.at[which, side],
                     recv_sems.at[which, 1 - side], device).start()
            elif do == "recv":
                copy(src, dst(side), send_sems.at[which, side],
                     recv_sems.at[which, side], device).wait_recv()
            else:
                copy(src, dst(1 - side), send_sems.at[which, side],
                     recv_sems.at[which, 1 - side], device).wait_send()

    def parent_halo(side, do):
        halo(x_side, side, parent.at[0 if side == LOW else prows - 1],
             lambda where: prow.at[where], row_s, row_r, 0, do)
        halo(y_side, side, pcol_send.at[side], lambda where: pcol.at[where], col_s, col_r, 0, do)

    def nest_halo(turn, side, do, kinds=("x", "y")):
        if "x" in kinds:
            if turn == 0:
                src = nest.at[0 if side == LOW else nrows - 1]
            else:
                src = nrow_send.at[turn - 1, side]
            halo(x_side, side, src, lambda where: nrow.at[turn, where], row_s, row_r, 1 + turn, do)
        if "y" in kinds:
            halo(y_side, side, ncol_send.at[turn, side], lambda where: ncol.at[turn, where],
                 col_s, col_r, 1 + turn, do)

    def peer(k):
        return {"gx": lax.rem(me + k, n_x)}

    def key_copy(k):
        return copy(keys.at[0], keys.at[k], key_s.at[k], key_r.at[k], peer(k))

    def answer_copy(k):
        return copy(answers_send.at[k], answers.at[k], ans_s.at[k], ans_r.at[k],
                    {"gx": lax.rem(me + (n_x - k), n_x)})

    def mean_copy(k):
        return copy(means.at[0], means.at[k], mean_s.at[k], mean_r.at[k], peer(k))

    for side in (LOW, HIGH):
        parent_halo(side, "start")
    over(1, n_x, lambda k: key_copy(k).start())
    for side in (LOW, HIGH):
        nest_halo(0, side, "start")

    for r in range(prows):
        centre = parent[r].astype(F32)
        around = inside(centre, pcols)
        if r > 0:
            around = around + parent[r - 1].astype(F32)
        if r < prows - 1:
            around = around + parent[r + 1].astype(F32)
        stepped[r] = mix(centre + nu_parent_c * (around - 4.0 * centre))
    for side in (LOW, HIGH):
        parent_halo(side, "recv")
    row_low, row_high, col_low, col_high = from_halos(parent_lhs, prow, pcol)
    stepped[0] = stepped[0] + row_low
    stepped[prows - 1] = stepped[prows - 1] + row_high
    for r in range(prows):
        add_cols(stepped.at[r], r, pcols, col_low, col_high)
        stepped_bf[r * levels:(r + 1) * levels, :] = stepped[r].astype(BF16)

    parent_col = lax.broadcasted_iota(jnp.int32, (pcols, blocks), 0)
    shift = pcols.bit_length() - 1

    def row_of(k):
        return lax.shift_right_arithmetic(keys[k, 0:1, :] - me * (prows * pcols), shift)

    def places(k):
        return row_of(k), one_hot(parent_col == (keys[k, 0:1, :] & (pcols - 1)))

    parent_across = lax.broadcasted_iota(jnp.int32, (blocks, pcols), 1)

    def place_back(k):
        down = jnp.transpose(keys[k])[:, 0:1]
        back[k] = one_hot(parent_across == (down & (pcols - 1)))

    def serve(k):
        if not (isinstance(k, int) and k == 0):
            key_copy(k).wait_recv()
        row, hot = places(k)
        found = dot(stepped_bf[...], hot)
        total = jnp.zeros((levels, blocks), F32)
        for r in range(prows):
            total = jnp.where(row == r, found[r * levels:(r + 1) * levels], total)
        if isinstance(k, int) and k == 0:
            answers[0] = total.astype(BF16)
        else:
            answers_send[k] = total.astype(BF16)
            answer_copy(k).start()

    over(1, n_x, serve)
    serve(0)

    def weight(low_row):
        first = nest_of[lax.rem(low_row + total_rows, total_rows)]
        second = nest_of[lax.rem(low_row + 1, total_rows)]
        return jnp.where(first == second, 1.0, 0.0).astype(F32)

    weights = [weight(me * nrows + r - 1) for r in range(nrows + 1)]

    def diffuse(get, put):
        for r in range(nrows):
            centre = get(r)
            around = inside(centre, ncols)
            if r > 0:
                around = around + get(r - 1) * weights[r]
            if r < nrows - 1:
                around = around + get(r + 1) * weights[r + 1]
            put(r, mix(keep_c * (centre + nu_nest_c * (around - 4.0 * centre))))

    def nest_halos(turn):
        for side in (LOW, HIGH):
            nest_halo(turn, side, "recv")
        row_low, row_high, col_low, col_high = from_halos(nest_lhs, nrow.at[turn], ncol.at[turn])
        return row_low * weights[0], row_high * weights[nrows], col_low, col_high

    def put_state(r, value):
        state[0, r] = value

    diffuse(lambda r: nest[r].astype(F32), put_state)
    row_low, row_high, col_low, col_high = nest_halos(0)
    state[0, 0] = state[0, 0] + row_low
    state[0, nrows - 1] = state[0, nrows - 1] + row_high
    for r in range(nrows):
        add_cols(state.at[0, r], r, ncols, col_low, col_high)

    parent_row = lax.broadcasted_iota(jnp.int32, (16, blocks), 0)
    over(0, n_x, place_back)

    def count_step(k):
        return dot(one_hot(parent_row == row_of(k)), back[k])

    forced = answers[0].astype(F32)
    if n_x <= 8:
        counts = count_step(0)
        for k in range(1, n_x):
            counts = counts + count_step(k)
        for k in range(1, n_x):
            answer_copy(k).wait_recv()
            forced = forced + answers[k].astype(F32)
    else:
        counts = lax.fori_loop(
            0, n_x, lambda k, t: t + count_step(k), jnp.zeros((16, pcols), F32))

        def collect(k, t):
            answer_copy(k).wait_recv()
            return t + answers[k].astype(F32)

        forced = lax.fori_loop(1, n_x, collect, forced)

    block_at = lax.broadcasted_iota(jnp.int32, (bcols, ncols), 0)
    cell_at = lax.broadcasted_iota(jnp.int32, (bcols, ncols), 1)
    spread = one_hot((cell_at >= 3 * block_at) & (cell_at < 3 * block_at + 3))
    spread2 = jnp.concatenate([spread, spread], axis=0)
    drive = mix(relax_c * forced)
    for a in range(brows):
        high, low = split(drive[:, a * bcols:(a + 1) * bcols])
        pulled[a] = dot(jnp.concatenate([high, low], axis=1), spread2)

    def send_rows(turn, r, value):
        side = LOW if r == 0 else HIGH
        nrow_send[turn - 1, side] = value.astype(BF16)
        nest_halo(turn, side, "start", ("x",))

    for r in (0, nrows - 1, *range(1, nrows - 1)):
        value = state[0, r] + pulled[r // 3]
        state[0, r] = value
        if r in (0, nrows - 1):
            send_rows(1, r, value)
    for side, packed in enumerate(edges([state[0, r] for r in range(nrows)], ncols)):
        ncol_send[1, side] = packed.astype(BF16)
        nest_halo(1, side, "start", ("y",))

    for turn in range(1, TURNS):
        now, later = (turn - 1) % 2, turn % 2

        def put_next(r, value):
            state[later, r] = value + pulled[r // 3]

        diffuse(lambda r: state[now, r], put_next)
        ends = None
        if turn < TURNS - 1:
            ends = edges([state[later, r] for r in range(nrows)], ncols)
        row_low, row_high, col_low, col_high = nest_halos(turn)
        for r, added in ((0, row_low), (nrows - 1, row_high)):
            state[later, r] = state[later, r] + added
            add_cols(state.at[later, r], r, ncols, col_low, col_high)
            if turn < TURNS - 1:
                send_rows(turn + 1, r, state[later, r])
        if turn < TURNS - 1:
            for side, (end, at, own) in enumerate(
                zip(ends, (0, ncols - 1), (col_low, col_high))
            ):
                end = end + own
                end = end + jnp.where(lane128 == 0, row_low[:, at:at + 1], 0.0)
                end = end + jnp.where(lane128 == nrows - 1, row_high[:, at:at + 1], 0.0)
                ncol_send[turn + 1, side] = end.astype(BF16)
                nest_halo(turn + 1, side, "start", ("y",))
        for r in range(1, nrows - 1):
            add_cols(state.at[later, r], r, ncols, col_low, col_high)

    last = (TURNS - 1) % 2
    down_cell = lax.broadcasted_iota(jnp.int32, (ncols, bcols), 0)
    down_block = lax.broadcasted_iota(jnp.int32, (ncols, bcols), 1)
    gather_up = one_hot((down_cell >= 3 * down_block) & (down_cell < 3 * down_block + 3))
    for a in range(brows):
        summed = state[last, 3 * a] + state[last, 3 * a + 1] + state[last, 3 * a + 2]
        high, low = split(summed)
        both = dot(jnp.concatenate([high, low], axis=0), gather_up)
        mean = (both[:levels] + both[levels:]) * (1.0 / 9.0)
        means[0, :, a * bcols:(a + 1) * bcols] = mean.astype(BF16)
    over(1, n_x, lambda k: mean_copy(k).start())
    for r in range(nrows):
        nest_out[r] = state[last, r].astype(BF16)
    store_nest = pltpu.make_async_copy(nest_out, nest_out_h, out_sem)
    store_nest.start()

    def give(k, total):
        row = row_of(k)
        mean = means[k].astype(F32)
        shared = jnp.concatenate(
            [jnp.where(row == r, mean, 0.0).astype(BF16) for r in range(prows)], axis=0
        )
        return total + dot(shared, back[k])

    for r in range(prows):
        stepped[r] = stepped[r] * (1.0 - feedback_c * counts[r:r + 1, :])
    returned = give(0, jnp.zeros((prows * levels, pcols), F32))
    if n_x <= 8:
        for k in range(1, n_x):
            mean_copy(k).wait_recv()
            returned = give(k, returned)
    else:
        def give_next(k, total):
            mean_copy(k).wait_recv()
            return give(k, total)

        returned = lax.fori_loop(1, n_x, give_next, returned)
    for r in range(prows):
        given = returned[r * levels:(r + 1) * levels]
        whole_row = stepped[r] + feedback_c * given
        for h in range(pcols // 128):
            turned[h, pl.ds(r, levels, stride=prows), :] = whole_row[:, h * 128:(h + 1) * 128]
    for h in range(pcols // 128):
        parent_out[:, :, h * 128:(h + 1) * 128] = turned[h].reshape(
            levels, prows, 128).astype(BF16)

    for side in (LOW, HIGH):
        parent_halo(side, "send")
        for turn in range(TURNS):
            nest_halo(turn, side, "send")

    def sent(k):
        key_copy(k).wait_send()
        answer_copy(k).wait_send()
        mean_copy(k).wait_send()

    over(1, n_x, sent)
    store_nest.wait()


def hand_over(parent, nest, parent_out, nest_out, parent_held, nest_held, in_sem, out_sem):
    coming, going = [], []
    for source, held, target in (
        (parent, parent_held, parent_out), (nest, nest_held, nest_out)
    ):
        half = source.shape[0] // 2
        for first in (0, half):
            part = pl.ds(first, half)
            i = len(coming)
            coming.append(
                pltpu.make_async_copy(source.at[part], held.at[part], in_sem.at[i]))
            going.append(
                pltpu.make_async_copy(held.at[part], target.at[part], out_sem.at[i]))
    for come in coming:
        come.start()
    for come, go in zip(coming, going):
        come.wait()
        go.start()
    for go in going:
        go.wait()


def body(n_x, n_gy, n_gz, parent, nest, nu_p, nu_n, relax, feedback, vert_mix, owner, cell, nest_of):
    levels, prows, pcols = parent.shape
    _, nrows, ncols = nest.shape
    blocks = cell.size
    vmem = pl.BlockSpec(memory_space=pltpu.VMEM)
    dma = pltpu.SemaphoreType.DMA
    parent_out, nest_out = pl.pallas_call(
        functools.partial(kernel, n_x, n_gy, n_gz),
        out_shape=(
            jax.ShapeDtypeStruct((levels, prows, pcols), BF16),
            jax.ShapeDtypeStruct((nrows, levels, ncols), BF16),
        ),
        in_specs=[pl.BlockSpec(memory_space=pltpu.HBM)] * 10,
        out_specs=(vmem, pl.BlockSpec(memory_space=pltpu.HBM)),
        scratch_shapes=[
            pltpu.VMEM(parent.shape, BF16),
            pltpu.VMEM((nrows, levels, ncols), BF16),
            *[pltpu.VMEM((1, levels), F32)] * 4,
            pltpu.VMEM((levels, levels), F32),
            *[pltpu.VMEM((1, blocks), jnp.int32)] * 2,
            pltpu.SMEM(nest_of.shape, jnp.int32),
            pltpu.VMEM((pcols // 128, levels * prows, 128), F32),
            pltpu.VMEM((prows, levels, pcols), BF16),
            dma((10,)),
            pltpu.VMEM((nrows, levels, ncols), BF16),
            dma,
            pltpu.VMEM((n_x, 8, blocks), jnp.int32),
            pltpu.VMEM((2, levels, pcols), BF16),
            pltpu.VMEM((2, levels, 128), BF16),
            pltpu.VMEM((2, levels, 128), BF16),
            pltpu.VMEM((TURNS, 2, levels, ncols), BF16),
            pltpu.VMEM((TURNS - 1, 2, levels, ncols), BF16),
            pltpu.VMEM((TURNS, 2, levels, 128), BF16),
            pltpu.VMEM((TURNS, 2, levels, 128), BF16),
            pltpu.VMEM((2, nrows, levels, ncols), F32),
            pltpu.VMEM((prows, levels, pcols), F32),
            pltpu.VMEM((prows * levels, pcols), BF16),
            pltpu.VMEM((n_x, levels, blocks), BF16),
            pltpu.VMEM((n_x, levels, blocks), BF16),
            pltpu.VMEM((n_x, levels, blocks), BF16),
            pltpu.VMEM((levels, 3 * levels), BF16),
            pltpu.VMEM((nrows // 3, levels, ncols), F32),
            pltpu.VMEM((n_x, blocks, pcols), BF16),
            dma((1 + TURNS, 2)), dma((1 + TURNS, 2)), dma((1 + TURNS, 2)), dma((1 + TURNS, 2)),
            dma((n_x,)), dma((n_x,)), dma((n_x,)), dma((n_x,)), dma((n_x,)), dma((n_x,)),
        ],
        compiler_params=pltpu.CompilerParams(
            collective_id=0, has_side_effects=True, vmem_limit_bytes=62 * 1024 * 1024
        ),
    )(
        parent, nest.transpose(1, 0, 2),
        nu_p.reshape(1, -1), nu_n.reshape(1, -1), relax.reshape(1, -1), feedback.reshape(1, -1),
        vert_mix, owner.reshape(1, -1), cell.reshape(1, -1), nest_of,
    )
    hbm = pl.BlockSpec(memory_space=pltpu.HBM)
    parent_out, nest_out = pl.pallas_call(
        hand_over,
        out_shape=(
            jax.ShapeDtypeStruct(parent_out.shape, BF16),
            jax.ShapeDtypeStruct(nest_out.shape, BF16),
        ),
        in_specs=[hbm, hbm],
        out_specs=(hbm, hbm),
        scratch_shapes=[
            pltpu.VMEM(parent_out.shape, BF16), pltpu.VMEM(nest_out.shape, BF16),
            dma((4,)), dma((4,)),
        ],
        compiler_params=pltpu.CompilerParams(vmem_limit_bytes=62 * 1024 * 1024),
    )(parent_out, nest_out)
    return parent_out, nest_out.transpose(1, 0, 2)


def solution(mesh):
    sizes = mesh.shape
    grid = P("groups", "gx", ("gy", "gz"))
    placed = (
        grid, grid, P(), P(), P(), P(), P(),
        P("gx", ("gy", "gz"), None, None), P("gx", ("gy", "gz"), None), P(),
    )
    return jax.shard_map(
        functools.partial(body, sizes["gx"], sizes["gy"], sizes["gz"]),
        mesh=mesh,
        in_specs=placed,
        out_specs=(grid, grid),
        check_vma=False,
    )
```
